128 devices in a mesh: batch: 32 (over z, y, core), head: 4 (over x).
Axes of the slice: x: 4, y: 4, z: 4, core: 2. Of those that a mesh axis runs over, the one named last changes fastest.
Arguments:
- item_ids: int32 [32, 1024], P('batch'), may hold values from 0 to 131071, as said below
- lengths: int32 [32], P('batch'), may hold values from 1 to 1024, as said below
- assignment: int32 [32], P('batch'), may hold values from 0 to 31, as said below
- row_of_item: int32 [131072], replicated, may hold values from 0 to 131071, as said below
- table_values: bfloat16 [131072, 1024], P('batch', 'head'), may hold values from -6 to 6
- row_scale: float32 [131072], P('batch'), may hold values from 0.3 to 3
- row_bias: float32 [131072], P('batch'), may hold values from -4 to 4
- proj_weight: bfloat16 [1024, 4096], P(None, 'head'), may hold values from -0.1875 to 0.1875
- out_weight: bfloat16 [1024, 1024], P('head'), may hold values from -0.1875 to 0.1875
- cotangent: bfloat16 [32768, 1024], P('batch', 'head'), may hold values from -6 to 6
Outputs:
- layer_out: bfloat16 [32768, 1024], P('batch', 'head')
- row_grad: float32 [131072, 1024], P('batch', 'head')
- proj_grad: float32 [1024, 4096], P(None, 'head')
- out_grad: float32 [1024, 1024], P('head')
The draws below stay inside these ranges and needn't reach their ends.
Inputs may be any that keep to these rules, and one draw needn't show every extreme that they name: `item_ids`: counting all 1024 positions (past its length too) of the history that assignment places on a batch index, at most 64 have their row stored on any one batch index (row // 4096), and for every history some storing index is reached exactly 64 times. `lengths`: some history has length 1024. A permutation: history h is computed in slot assignment[h], which lies on batch index assignment[h]. `row_of_item`: A permutation of the table rows.
All inputs are finite; a program needn't handle non-finite values.
Results may differ from the reference program's by a relative error of at most 0.012.
The reference program's roundings to bfloat16 on the way (of `embedded`, `normed_low`, `activated`, `weights`, `gated`, `grad_attended`, `grad_scores` and `grad_projected`) count: a program that leaves them out, or rounds other values in their place, can miss the bound.
Values may be sent and summed in bfloat16 or wider, within the bound.
No kernel may reach another device: no remote copies, remote signals or barrier semaphores. Data moves between devices by JAX's collectives and lax.ppermute only.
A program may use at most 128 MiB of HBM per device.

```python
import math
import jax
import jax.numpy as jnp
from jax import lax

D = 1024
HEADS = 16
HD = 64
MAXLEN = 1024
HIST_DEV = 1
ITEMS_DEV = 4096
HISTS = 32
ITEMS = 131072
EVENTS = 32768


def shared_layout(key):
    length_key, pick_key, device_key, row_key, owner_key, event_key = jax.random.split(key, 6)
    batch_total = HISTS // HIST_DEV
    short_lengths = jax.random.randint(jax.random.fold_in(length_key, 1), (HISTS,), 1, MAXLEN // 4 + 1)
    long_lengths = jax.random.randint(jax.random.fold_in(length_key, 2), (HISTS,), 1, MAXLEN + 1)
    chooser = jax.random.randint(jax.random.fold_in(length_key, 3), (HISTS,), 0, 4)
    lengths = jnp.where(chooser == 0, long_lengths, short_lengths)
    longest = jax.random.randint(pick_key, (), 0, HISTS)
    history_order = jnp.arange(HISTS, dtype=jnp.int32)
    lengths = jnp.where(history_order == longest, MAXLEN, lengths).astype(jnp.int32)
    ranking = jnp.argsort(-lengths, stable=True)
    round_number = history_order // batch_total
    within_round = history_order % batch_total
    column = jnp.where(round_number % 2 == 0, within_round, batch_total - 1 - within_round)
    devices = jax.random.permutation(device_key, batch_total).astype(jnp.int32)
    slot_of_rank = (devices[column] * HIST_DEV + round_number).astype(jnp.int32)
    assignment = jnp.zeros((HISTS,), jnp.int32).at[ranking].set(slot_of_rank)
    row_of_item = jax.random.permutation(row_key, ITEMS).astype(jnp.int32)
    item_of_row = jnp.argsort(row_of_item).astype(jnp.int32)
    cap_history = 2 * MAXLEN // batch_total
    pool_size = 2 * MAXLEN
    stars = jax.random.randint(owner_key, (batch_total,), 0, batch_total)

    def one_slot(slot_key, star):
        first_key = jax.random.fold_in(slot_key, 1)
        second_key = jax.random.fold_in(slot_key, 2)
        third_key = jax.random.fold_in(slot_key, 3)
        fourth_key = jax.random.fold_in(slot_key, 4)
        priority = jax.random.permutation(first_key, pool_size).astype(jnp.int32)
        pool_index = jnp.arange(pool_size, dtype=jnp.int32)
        score = priority + jnp.where(pool_index < cap_history, pool_size, 0)
        chosen = jnp.argsort(-score, stable=True)[:MAXLEN].astype(jnp.int32)
        owners = (chosen // cap_history + star) % batch_total
        owners = owners[jax.random.permutation(second_key, MAXLEN)]
        local_row = jnp.minimum(jax.random.randint(third_key, (MAXLEN,), 0, ITEMS_DEV), jax.random.randint(fourth_key, (MAXLEN,), 0, ITEMS_DEV))
        return (owners * ITEMS_DEV + local_row).astype(jnp.int32)
    slot_keys = jax.random.split(event_key, HISTS)
    slot_stars = stars[jnp.arange(HISTS, dtype=jnp.int32) // HIST_DEV]
    table_rows = jax.vmap(one_slot)(slot_keys, slot_stars)
    processed_ids = item_of_row[table_rows]
    item_ids = processed_ids[assignment].astype(jnp.int32)
    return (item_ids, lengths, assignment, row_of_item)


def draw_item_ids(key, part):
    return shared_layout(key)[0]


def draw_lengths(key, part):
    return shared_layout(key)[1]


def draw_assignment(key, part):
    return shared_layout(key)[2]


def draw_row_of_item(key, part):
    return shared_layout(key)[3]


def level_of(rng, dims, shards, smallest, largest):
    def one(dim, parts):
        draws = jax.random.uniform(jax.random.fold_in(jax.random.fold_in(rng, 6), dim), (parts,), jnp.float32, smallest / len(shards), largest / len(shards))
        return jnp.repeat(jnp.exp(draws), dims[dim] // parts).reshape((-1,) + (1,) * (len(dims) - dim - 1))

    factor_of = one(*shards[0])
    for cut in shards[1:]:
        factor_of = factor_of * one(*cut)
    return factor_of


def bell_draw(own_key, dims, width, limit, cuts=(), held_as=jnp.bfloat16):
    result = jax.random.normal(own_key, dims, jnp.float32) * width
    if len(cuts) > 0:
        result = level_of(own_key, dims, cuts, -0.22, 0.18) * result
    return jnp.clip(result, min=-limit, max=limit).astype(held_as)


def setup_inputs(seed: int = 0) -> dict:
    seeds = jax.random.split(jax.random.key(seed), 11)
    return {
        "item_ids": draw_item_ids(jax.random.fold_in(seeds[10], 71), 0),
        "lengths": draw_lengths(jax.random.fold_in(seeds[10], 71), 0),
        "assignment": draw_assignment(jax.random.fold_in(seeds[10], 71), 0),
        "row_of_item": draw_row_of_item(jax.random.fold_in(seeds[10], 71), 0),
        "table_values": bell_draw(seeds[4], (ITEMS, D), 1.0, 6.0, ((0, 32), (1, 4))),
        "row_scale": jnp.clip(jnp.exp(math.log(3.0) - 2.3025851 * jax.random.uniform(seeds[5], (ITEMS,), jnp.float32) ** level_of(seeds[5], (ITEMS,), ((0, 32),), -0.2, 0.2)), 0.3, 3.0),
        "row_bias": bell_draw(seeds[6], (ITEMS,), 1.0, 4.0, ((0, 32),), jnp.float32),
        "proj_weight": bell_draw(seeds[7], (D, 4 * D), D ** -0.5, 0.1875, ((1, 4),)),
        "out_weight": bell_draw(seeds[8], (D, D), D ** -0.5, 0.1875, ((0, 4),)),
        "cotangent": bell_draw(seeds[9], (EVENTS, D), 1.0, 6.0, ((0, 32), (1, 4))),
    }


epsilon = 1e-05

def silu_slope(values):
    sigma = jax.nn.sigmoid(values)
    return sigma * (1.0 + values * (1.0 - sigma))

def widen(values):
    return lax.optimization_barrier(values).astype(jnp.float32)

def one_history(running, inputs, proj_weight, out_weight):
    proj_total, out_total = running
    embedded, upstream, alive_rows, length = inputs
    scale_qk = HD ** (-0.5)
    features = embedded.astype(jnp.float32)
    centred = features - lax.optimization_barrier(jnp.mean(features, axis=1, keepdims=True))
    inverse_std = lax.rsqrt(lax.optimization_barrier(jnp.mean(centred * centred, axis=1, keepdims=True)) + epsilon)
    normed = centred * inverse_std
    normed_low = normed.astype(jnp.bfloat16)
    projected = jnp.dot(normed_low, proj_weight, preferred_element_type=jnp.float32)
    activated = jax.nn.silu(projected).astype(jnp.bfloat16).reshape(MAXLEN, HEADS, 4, HD)
    gate_part = activated[:, :, 0, :].astype(jnp.float32)
    value_part = activated[:, :, 1, :].astype(jnp.float32)
    query_part = activated[:, :, 2, :].astype(jnp.float32)
    key_part = activated[:, :, 3, :].astype(jnp.float32)
    positions = jnp.arange(MAXLEN, dtype=jnp.int32)
    allowed = ((positions[None, :] <= positions[:, None]) & (positions[:, None] < length)).astype(jnp.float32)[None]
    scores = jnp.einsum('ihd,jhd->hij', query_part, key_part) * scale_qk
    weights = widen((jax.nn.silu(scores) * allowed).astype(jnp.bfloat16))
    attended = jnp.einsum('hij,jhd->ihd', weights, value_part).reshape(MAXLEN, D)
    av_centred = attended - lax.optimization_barrier(jnp.mean(attended, axis=1, keepdims=True))
    av_inverse = lax.rsqrt(lax.optimization_barrier(jnp.mean(av_centred * av_centred, axis=1, keepdims=True)) + epsilon)
    normal_av = av_centred * av_inverse
    gate_flat = gate_part.reshape(MAXLEN, D)
    gated = (normal_av * gate_flat).astype(jnp.bfloat16)
    mixed = features + jnp.dot(gated, out_weight, preferred_element_type=jnp.float32)
    layer_rows = mixed.astype(jnp.bfloat16)
    out_total = out_total + jnp.dot(gated.T, upstream, preferred_element_type=jnp.float32)
    grad_gated = jnp.dot(upstream, out_weight.T, preferred_element_type=jnp.float32)
    grad_normal = grad_gated * gate_flat
    grad_gate = grad_gated * normal_av
    grad_attended = alive_rows[:, None] * av_inverse * (grad_normal - lax.optimization_barrier(jnp.mean(grad_normal, axis=1, keepdims=True)) - normal_av * lax.optimization_barrier(jnp.mean(grad_normal * normal_av, axis=1, keepdims=True)))
    grad_attended = widen(grad_attended.astype(jnp.bfloat16)).reshape(MAXLEN, HEADS, HD)
    grad_value = jnp.einsum('hij,ihd->jhd', weights, grad_attended)
    grad_weights = jnp.einsum('ihd,jhd->hij', grad_attended, value_part)
    grad_scores = widen((grad_weights * silu_slope(scores) * allowed * scale_qk).astype(jnp.bfloat16))
    grad_query = jnp.einsum('hij,jhd->ihd', grad_scores, key_part)
    grad_key = jnp.einsum('hij,ihd->jhd', grad_scores, query_part)
    grad_act = jnp.stack([grad_gate.reshape(MAXLEN, HEADS, HD), grad_value, grad_query, grad_key], axis=2).reshape(MAXLEN, 4 * D)
    grad_projected = (grad_act * silu_slope(projected)).astype(jnp.bfloat16)
    proj_total = proj_total + jnp.dot(normed_low.T, grad_projected, preferred_element_type=jnp.float32)
    grad_normed = jnp.dot(grad_projected, proj_weight.T, preferred_element_type=jnp.float32)
    grad_embedded = alive_rows[:, None] * (upstream.astype(jnp.float32) + inverse_std * (grad_normed - lax.optimization_barrier(jnp.mean(grad_normed, axis=1, keepdims=True)) - normed * lax.optimization_barrier(jnp.mean(grad_normed * normed, axis=1, keepdims=True))))
    return ((proj_total, out_total), (layer_rows, grad_embedded))

def reference(item_ids, lengths, assignment, row_of_item, table_values, row_scale, row_bias, proj_weight, out_weight, cotangent):
    slot_order = jnp.arange(HISTS, dtype=jnp.int32)
    source = jnp.zeros((HISTS,), jnp.int32).at[assignment].set(slot_order)
    slot_lengths = lengths[source]
    positions = jnp.arange(MAXLEN, dtype=jnp.int32)
    alive_rows = (positions[None, :] < slot_lengths[:, None]).astype(jnp.float32)
    table_rows = row_of_item[item_ids[source].reshape(-1)]
    dequant = table_values[table_rows].astype(jnp.float32) * row_scale[table_rows][:, None] + row_bias[table_rows][:, None]
    embedded = (dequant * alive_rows.reshape(-1)[:, None]).astype(jnp.bfloat16)
    initial = (jnp.zeros((D, 4 * D), jnp.float32), jnp.zeros((D, D), jnp.float32))

    def history_step(running, inputs):
        return one_history(running, inputs, proj_weight, out_weight)
    totals, outputs = lax.scan(history_step, initial, (embedded.reshape(HISTS, MAXLEN, D), cotangent.reshape(HISTS, MAXLEN, D), alive_rows, slot_lengths))
    layer_rows, grad_embedded = outputs
    row_grad = jnp.zeros((ITEMS, D), jnp.float32).at[table_rows].add(grad_embedded.reshape(EVENTS, D))
    return (layer_rows.reshape(EVENTS, D), row_grad, totals[0], totals[1])
```

```python
import jax
import jax.numpy as jnp
from jax import lax
from jax.experimental import pallas as pl
from jax.experimental.pallas import tpu as pltpu
from jax.sharding import Mesh, PartitionSpec as P

HD = 64
EV = 1024
WIDTH = 256
OWNERS = 32
CAP = 64
ROWS = 4096
BATCH = ("z", "y", "core")
epsilon = 1e-05
F32 = jnp.float32
BF16 = jnp.bfloat16
I32 = jnp.int32


def iota(shape, axis):
    return lax.broadcasted_iota(I32, shape, axis)


def one(mask):
    return jnp.where(mask, 1.0, 0.0).astype(BF16)


def mm(a, b, ca=1, cb=0):
    return lax.dot_general(a, b, (((ca,), (cb,)), ((), ())), preferred_element_type=F32)


def low(x):
    return x.astype(F32).astype(BF16)


def call(body, outs, memory=None, scratch=(), mib=60, **kw):
    spec = pl.BlockSpec(memory_space=pltpu.VMEM)
    smem = pl.BlockSpec(memory_space=pltpu.SMEM)
    single = not isinstance(outs, (tuple, list))
    out_list = [outs] if single else list(outs)

    def run(*args):
        in_specs = [smem if memory and i in memory else spec for i in range(len(args))]
        result = pl.pallas_call(
            body,
            out_shape=out_list,
            in_specs=in_specs,
            out_specs=[spec] * len(out_list),
            scratch_shapes=list(scratch),
            compiler_params=pltpu.CompilerParams(vmem_limit_bytes=mib * 2**20),
            **kw,
        )(*args)
        return result[0] if single else result

    return run


def sds(shape, dtype):
    return jax.ShapeDtypeStruct(shape, dtype)


def route_body(length_ref, slot_ref, ids_ref, rows_ref, out_ref):
    ids = ids_ref[...]
    high, lane = ids >> 7, ids & 127
    table = rows_ref[...]
    pieces = jnp.concatenate([low(table & 255), low((table >> 8) & 255), low(table >> 16)], axis=1)
    picked = mm(pieces, one(iota((EV, EV), 0) == high), 0, 0)
    value = picked[0:128] + 256.0 * picked[128:256] + 65536.0 * picked[256:384]
    row = jnp.sum(
        jnp.where(iota((128, EV), 0) == lane, value, 0.0), axis=0, keepdims=True
    ).astype(I32)
    owner, local = row >> 12, (row & 4095) + 1
    alive = iota((1, EV), 1) < length_ref[0]
    hits = (iota((OWNERS, EV), 0) == owner) & alive
    hit = jnp.where(hits, 1.0, 0.0)
    before = mm(hit.astype(BF16), one(iota((EV, EV), 0) < iota((EV, EV), 1)))
    arrival = jnp.sum(hit * before, axis=0, keepdims=True).astype(I32)
    parts = jnp.concatenate(
        [hit * (local & 127).astype(F32), hit * (local >> 7).astype(F32)], axis=0
    ).astype(BF16)
    asked = mm(parts, one(iota((CAP, EV), 0) == arrival), 1, 1)
    asked = (asked[0:OWNERS] + 128.0 * asked[OWNERS:]).astype(I32)
    slot = slot_ref[0]
    first = jnp.concatenate([asked, jnp.full((OWNERS, 64), slot, I32)], axis=1)
    place = jnp.where(alive, owner * CAP + arrival + 1, 0)
    packed = place[:, 0:512] + 4096 * place[:, 512:1024]
    level = iota((8, 128), 0)
    base = jnp.zeros((8, 128), I32)
    for r in range(4):
        piece = jnp.broadcast_to(packed[:, 128 * r : 128 * r + 128], (8, 128))
        base = jnp.where(level == r + 1, piece, base)
    for d in range(OWNERS):
        head_row = jnp.broadcast_to(first[d : d + 1, :], (8, 128))
        out_ref[d] = jnp.where(level == 0, head_row, jnp.where(slot == d, base, 0))


def fetch_body(asked_ref, table_ref, scale_ref, bias_ref, rows_ref, order_ref, hot_ref):
    first = jnp.concatenate([asked_ref[h, 0:1, :] for h in range(OWNERS)], axis=0)
    slot = first[:, 64:65]
    lane = iota((OWNERS, 128), 1)
    small, large = low(first & 127), low(first >> 7)
    place = one(lane == slot)
    columns = (mm(small, place, 0, 0) + 128.0 * mm(large, place, 0, 0)).astype(I32) - 1
    even, odd = one(2 * lane == slot), one(2 * lane + 1 == slot)
    even_rows = mm(even, small, 0, 0) + 128.0 * mm(even, large, 0, 0)
    odd_rows = mm(odd, small, 0, 0) + 128.0 * mm(odd, large, 0, 0)
    order = jnp.where(iota((128, 128), 1) < 64, even_rows, pltpu.roll(odd_rows, 64, 1))
    order_ref[...] = order[0:16, :].astype(I32) - 1

    def split(x):
        a = x.astype(BF16).astype(F32)
        b = (x - a).astype(BF16).astype(F32)
        return [a, b, x - a - b]

    scale, bias = scale_ref[...], bias_ref[...]
    pieces = split(scale) + split(bias) + [jnp.zeros_like(scale)] * 2
    pieces = jnp.concatenate(pieces, axis=0).astype(BF16)
    table = table_ref[...]
    for c in range(4):
        for s in range(8):
            at = 8 * c + s
            hot_ref[64 * s : 64 * s + 64, :] = one(
                iota((CAP, ROWS), 1) == columns[0:64, at : at + 1]
            )
        hot = hot_ref[...]
        values = mm(hot, table)
        factors = mm(hot, pieces, 1, 1)
        scales = factors[:, 0:1] + factors[:, 1:2] + factors[:, 2:3]
        biases = factors[:, 3:4] + factors[:, 4:5] + factors[:, 5:6]
        rows_ref[512 * c : 512 * c + 512, :] = (values * scales + biases).astype(BF16)


def place_body(asked_ref, fetched_ref, out_ref, place_ref):
    packed = asked_ref[0]
    for h in range(1, OWNERS):
        packed = packed + asked_ref[h]
    packed = packed[1:5, :]
    place = jnp.concatenate([packed & 4095, packed >> 12], axis=0) - 1
    place_ref[...] = place
    full = jnp.concatenate([place.astype(F32), jnp.zeros((120, 128), F32)], axis=0)
    columns = full.T.astype(I32)
    fetched = fetched_ref[...]
    for b in range(8):
        hot = one(iota((128, OWNERS * CAP), 1) == columns[:, b : b + 1])
        rows = mm(hot, fetched).astype(BF16)
        for h in range(4):
            out_ref[h, 128 * b : 128 * b + 128, :] = rows


def head_tiles(act_ref, h):
    gates_values = act_ref[:, 256 * h : 256 * h + 128].astype(F32)
    query_key = act_ref[:, 256 * h + 128 : 256 * h + 256].astype(F32)
    lower = iota((EV, 128), 1) < 64
    if h % 2 == 0:
        value = jnp.where(lower, pltpu.roll(gates_values, 64, 1), 0.0)
        gate = jnp.where(lower, gates_values, 0.0)
    else:
        value = jnp.where(lower, 0.0, gates_values)
        gate = jnp.where(lower, 0.0, pltpu.roll(gates_values, 64, 1))
    key = jnp.where(lower, pltpu.roll(query_key, 64, 1), 0.0)
    return query_key, key, value, gate


def forward_body(
    x_ref, weight_ref, gg_ref, normed_ref, act_ref, slope_ref, istd_ref, att_ref, stats_ref, wt_ref
):
    weight = weight_ref[...]
    for b in range(4):
        rows = slice(256 * b, 256 * b + 256)
        x = [x_ref[h, rows, :].astype(F32) for h in range(4)]
        mean = sum(jnp.sum(v, axis=1, keepdims=True) for v in x) / 1024.0
        x = [v - mean for v in x]
        spread = sum(jnp.sum(v * v, axis=1, keepdims=True) for v in x) / 1024.0
        inverse = lax.rsqrt(spread + epsilon)
        istd_ref[rows, :] = inverse
        for h in range(4):
            normed_ref[rows, 256 * h : 256 * h + 256] = (x[h] * inverse).astype(BF16)
        half = 0.5 * mm(normed_ref[rows, :], weight)
        t = jnp.tanh(half)
        act_ref[rows, :] = (half + half * t).astype(BF16)
        slope_ref[rows, :] = (0.5 * (1.0 + t) * (1.0 + half * (1.0 - t))).astype(BF16)
    causal = iota((256, 256), 0) >= iota((256, 256), 1)
    gates = []
    for pair in range(2):
        gate_pair = None
        for h in (2 * pair, 2 * pair + 1):
            query_key, key, value, gate = head_tiles(act_ref, h)
            gate_pair = gate if gate_pair is None else gate_pair + gate
            left = (query_key * (1.0 / 16.0)).astype(BF16)
            key, value = key.astype(BF16), value.astype(BF16)
            for b in range(4):
                rows = slice(256 * b, 256 * b + 256)
                wt_ref[:, rows] = silu_masked(mm(left[rows], key[rows], 1, 1), causal)
                if b > 0:
                    wt_ref[:, 0 : 256 * b] = silu_masked(
                        mm(left[rows], key[0 : 256 * b], 1, 1), None
                    )
                total = mm(wt_ref[:, 0 : 256 * b + 256], value[0 : 256 * b + 256])
                cols = slice(128 * pair, 128 * pair + 128)
                if h % 2 == 0:
                    att_ref[rows, cols] = total
                else:
                    att_ref[rows, cols] += total
        gates.append(gate_pair)
    att = [att_ref[:, 0:128], att_ref[:, 128:256]]
    grad = [gg_ref[:, 0:128] * gates[0], gg_ref[:, 128:256] * gates[1]]
    mean = (jnp.sum(att[0], axis=1, keepdims=True) + jnp.sum(att[1], axis=1, keepdims=True)) / 256.0
    att = [v - mean for v in att]
    spread = sum(jnp.sum(v * v, axis=1, keepdims=True) for v in att)
    first = sum(jnp.sum(v, axis=1, keepdims=True) for v in grad)
    second = sum(jnp.sum(v * w, axis=1, keepdims=True) for v, w in zip(grad, att))
    lane = iota((EV, 128), 1)
    wide = jnp.where(
        lane == 0, mean, jnp.where(lane == 1, spread, jnp.where(lane == 2, first, second))
    )
    stats_ref[...] = wide.T[0:8, :]


def silu_masked(half, mask):
    result = half + half * jnp.tanh(half)
    if mask is not None:
        result = jnp.where(mask, result, 0.0)
    return result.astype(BF16)


def gate_body(
    stats_ref, att_ref, gg_ref, act_ref, out_weight_ref, gated_ref, da_ref, dgate_ref, mixed_ref
):
    stats = [stats_ref[h] for h in range(4)]
    mean = sum(s[0:1] for s in stats) / 4.0
    spread = sum(s[1:2] + 256.0 * (s[0:1] - mean) * (s[0:1] - mean) for s in stats) / 1024.0
    inverse = lax.rsqrt(spread + epsilon)
    first = sum(s[2:3] for s in stats) / 1024.0
    second = sum(s[3:4] + (s[0:1] - mean) * s[2:3] for s in stats) * inverse / 1024.0
    wide = jnp.concatenate([mean, inverse, first, second, jnp.zeros((124, EV), F32)], axis=0).T
    mean, inverse, first, second = (wide[:, i : i + 1] for i in range(4))
    lower = iota((EV, 128), 1) < 64
    for pair in range(2):
        cols = slice(128 * pair, 128 * pair + 128)
        even = act_ref[:, 512 * pair : 512 * pair + 128].astype(F32)
        odd = act_ref[:, 512 * pair + 256 : 512 * pair + 384].astype(F32)
        gate = jnp.where(lower, even, pltpu.roll(odd, 64, 1))
        normal = (att_ref[:, cols] - mean) * inverse
        gated_ref[:, cols] = (normal * gate).astype(BF16)
        up = gg_ref[:, cols]
        dgate_ref[:, cols] = up * normal
        da_ref[:, cols] = (inverse * (up * gate - first - normal * second)).astype(BF16)
    for b in range(4):
        rows = slice(256 * b, 256 * b + 256)
        mixed_ref[rows, :] = mm(gated_ref[rows, :], out_weight_ref[...]).astype(BF16)


def backward_body(
    act_ref,
    slope_ref,
    normed_ref,
    normed_t_ref,
    weight_t_ref,
    istd_ref,
    da_ref,
    dgate_ref,
    gated_t_ref,
    cot_ref,
    grads_ref,
    wgrad_ref,
    gp_ref,
    dq_ref,
):
    lower = iota((EV, 128), 1) < 64
    causal = iota((256, 256), 1) >= iota((256, 256), 0)
    for h in range(4):
        pair = h // 2
        query_key, key, value, _ = head_tiles(act_ref, h)
        left = query_key * (1.0 / 16.0)
        query = jnp.where(lower, 0.0, pltpu.roll(left, 64, 1)).astype(BF16)
        left = left.astype(BF16)
        key_t = (key * (1.0 / 16.0)).T.astype(BF16)
        key, value = key.astype(BF16), value.astype(BF16)
        da = da_ref[:, 128 * pair : 128 * pair + 128]
        dq_ref[...] = jnp.zeros_like(dq_ref)
        dks, dvs = [], []
        for b in range(4):
            keys = slice(256 * b, 256 * b + 256)
            dk = dv = 0.0
            spans = [(keys, causal)]
            if b < 3:
                spans.append((slice(256 * b + 256, EV), None))
            for span, mask in spans:
                half = mm(key[keys], left[span], 1, 1)
                t = jnp.tanh(half)
                weights = half + half * t
                up = mm(value[keys], da[span], 1, 1)
                gs = up * ((1.0 + t) * (1.0 + half - half * t))
                if mask is not None:
                    weights = jnp.where(mask, weights, 0.0)
                    gs = jnp.where(mask, gs, 0.0)
                gs = gs.astype(BF16)
                dv = dv + mm(weights.astype(BF16), da[span])
                dk = dk + mm(gs, query[span])
                dq_ref[:, span] += mm(key_t[:, keys], gs)
            dks.append(dk)
            dvs.append(dv)
        dqk = dq_ref[...].T + jnp.concatenate(dks, axis=0)
        dv = jnp.concatenate(dvs, axis=0)
        dgate = dgate_ref[:, 128 * pair : 128 * pair + 128]
        if h % 2 == 0:
            dgv = jnp.where(lower, dgate, pltpu.roll(dv, 64, 1))
        else:
            dgv = jnp.where(lower, pltpu.roll(dgate, 64, 1), dv)
        a, b = slice(256 * h, 256 * h + 128), slice(256 * h + 128, 256 * h + 256)
        gp_ref[:, a] = (dgv * slope_ref[:, a].astype(F32)).astype(BF16)
        gp_ref[:, b] = (dqk * slope_ref[:, b].astype(F32)).astype(BF16)
    for b in range(4):
        rows = slice(256 * b, 256 * b + 256)
        grad = mm(gp_ref[rows, :], weight_t_ref[...])
        normed = normed_ref[rows, :].astype(F32)
        first = jnp.sum(grad, axis=1, keepdims=True) / 1024.0
        second = jnp.sum(grad * normed, axis=1, keepdims=True) / 1024.0
        grad = (istd_ref[rows, :] * (grad - first - normed * second)).astype(BF16)
        for h in range(4):
            grads_ref[h, rows, :] = grad[:, 256 * h : 256 * h + 256]
    for b in range(4):
        rows = slice(256 * b, 256 * b + 256)
        wgrad_ref[rows, :] = mm(normed_t_ref[rows, :], gp_ref[...]).astype(BF16)
    wgrad_ref[EV : EV + 256, :] = mm(gated_t_ref[...], cot_ref[...]).astype(BF16)


def return_body(parts_ref, cot_ref, place_ref, out_ref):
    total = cot_ref[...].astype(F32)
    for h in range(4):
        total = total + parts_ref[h].astype(F32)
    total = total.astype(BF16)
    place = jnp.concatenate([place_ref[b : b + 1, :] for b in range(8)], axis=1)
    for c in range(4):
        hot = one(iota((512, EV), 0) + 512 * c == place)
        out_ref[512 * c : 512 * c + 512, :] = mm(hot, total).astype(BF16)


def scatter_body(rows_ref, order_ref, out_ref):
    order = jnp.concatenate([order_ref[b : b + 1, :] for b in range(16)], axis=1)
    base = pl.program_id(0) * 512
    hot = one(iota((512, OWNERS * CAP), 0) + base == order)
    out_ref[...] = mm(hot, rows_ref[...])


def scatter(rows, order):
    return pl.pallas_call(
        scatter_body,
        grid=(8,),
        out_shape=sds((ROWS, WIDTH), F32),
        in_specs=[
            pl.BlockSpec((OWNERS * CAP, WIDTH), lambda i: (0, 0)),
            pl.BlockSpec((16, 128), lambda i: (0, 0)),
        ],
        out_specs=pl.BlockSpec((512, WIDTH), lambda i: (i, 0)),
        compiler_params=pltpu.CompilerParams(vmem_limit_bytes=40 * 2**20),
    )(rows, order)


def shifted(x, axis, step):
    n = lax.axis_size(axis)
    return lax.ppermute(x, axis, [(i, (i + step) % n) for i in range(n)])


def reduce_blocks(x, axis):
    n = lax.axis_size(axis)
    me = lax.axis_index(axis)

    def block(step):
        return lax.dynamic_index_in_dim(x, (me + step) % n, 0, keepdims=False)

    arrived = [shifted(block(s), axis, s) for s in range(1, n)]
    total = block(0).astype(F32)
    for a in arrived:
        total = total + a.astype(F32)
    return total.astype(BF16)


def gather_blocks(x, axis):
    n = lax.axis_size(axis)
    me = lax.axis_index(axis)
    result = jnp.zeros((n,) + x.shape, x.dtype)
    for s in range(n):
        arrived = shifted(x, axis, s) if s else x
        result = lax.dynamic_update_index_in_dim(result, arrived, (me - s) % n, 0)
    return result


def shards(
    item_ids,
    lengths,
    assignment,
    row_of_item,
    table_values,
    row_scale,
    row_bias,
    proj_weight,
    out_weight,
    cotangent,
):
    portion = lax.all_gather(cotangent, "head", axis=1, tiled=True)
    payload = call(route_body, sds((OWNERS, 8, 128), I32), memory=(0, 1))(
        lengths, assignment, item_ids, row_of_item.reshape(1024, 128)
    )
    asked = lax.all_to_all(payload, BATCH, split_axis=0, concat_axis=0, tiled=True)
    rows, order = call(
        fetch_body,
        [sds((OWNERS * CAP, WIDTH), BF16), sds((16, 128), I32)],
        scratch=[pltpu.VMEM((512, ROWS), BF16)],
    )(asked, table_values, row_scale.reshape(1, ROWS), row_bias.reshape(1, ROWS))
    fetched = lax.all_to_all(
        rows.reshape(OWNERS, CAP, WIDTH), BATCH, split_axis=0, concat_axis=0, tiled=True
    ).reshape(OWNERS * CAP, WIDTH)
    copies, place = call(
        place_body, [sds((4, EV, WIDTH), BF16), sds((8, 128), I32)]
    )(asked, fetched)
    embedded = copies[0]
    features = lax.all_to_all(copies, "head", split_axis=0, concat_axis=0, tiled=True)
    grad_gated = mm(portion, out_weight, 1, 1)
    weight_t = proj_weight.T
    normed, act, slope, istd, att, stats = call(
        forward_body,
        [
            sds((EV, 1024), BF16),
            sds((EV, 1024), BF16),
            sds((EV, 1024), BF16),
            sds((EV, 1), F32),
            sds((EV, WIDTH), F32),
            sds((8, EV), F32),
        ],
        scratch=[pltpu.VMEM((256, EV), BF16)],
    )(features, proj_weight, grad_gated)
    every_stats = lax.all_to_all(
        jnp.broadcast_to(stats[None], (4, 8, EV)), "head", split_axis=0, concat_axis=0, tiled=True
    )
    normed_t = normed.T
    gated, grad_att, grad_gate, mixed = call(
        gate_body,
        [
            sds((EV, WIDTH), BF16),
            sds((EV, WIDTH), BF16),
            sds((EV, WIDTH), F32),
            sds((EV, 1024), BF16),
        ],
    )(every_stats, att, grad_gated, act, out_weight)
    mixed = lax.psum_scatter(mixed, "head", scatter_dimension=1, tiled=True)
    layer_out = (embedded.astype(F32) + mixed.astype(F32)).astype(BF16)
    grads, wgrad = call(
        backward_body,
        [sds((4, EV, WIDTH), BF16), sds((1280, 1024), BF16)],
        scratch=[pltpu.VMEM((EV, 1024), BF16), pltpu.VMEM((128, EV), F32)],
    )(act, slope, normed, normed_t, weight_t, istd, grad_att, grad_gate, gated.T, portion)
    parts = lax.all_to_all(grads, "head", split_axis=0, concat_axis=0, tiled=True)

    me = lax.axis_index("core")
    halves = wgrad.reshape(2, 640, 1024)
    sent = lax.dynamic_index_in_dim(halves, 1 - me, 0, keepdims=False)
    kept = lax.dynamic_index_in_dim(halves, me, 0, keepdims=False)
    half = (kept.astype(F32) + shifted(sent, "core", 1).astype(F32)).astype(BF16)
    quarter = reduce_blocks(half.reshape(4, 160, 1024), "y")
    piece = reduce_blocks(quarter.reshape(4, 40, 1024), "z")
    quarter = gather_blocks(piece, "z").reshape(160, 1024)
    half = gather_blocks(quarter, "y").reshape(640, 1024)
    other = shifted(half, "core", 1)
    first = jnp.where(me == 0, half, other)
    second = jnp.where(me == 0, other, half)
    proj_grad = jnp.concatenate([first, second[:384]], axis=0).astype(F32)
    out_grad = second[384:].astype(F32)

    outgoing = call(return_body, sds((OWNERS * CAP, WIDTH), BF16))(parts, cotangent, place)
    incoming = lax.all_to_all(
        outgoing.reshape(OWNERS, CAP, WIDTH), BATCH, split_axis=0, concat_axis=0, tiled=True
    ).reshape(OWNERS * CAP, WIDTH)
    row_grad = scatter(incoming, order)
    return (layer_out, row_grad, proj_grad, out_grad)


def solution(mesh):
    fine = Mesh(mesh.devices.reshape(4, 4, 2, 4), BATCH + ("head",))
    placed = (
        P(BATCH, None),
        P(BATCH),
        P(BATCH),
        P(),
        P(BATCH, "head"),
        P(BATCH),
        P(BATCH),
        P(None, "head"),
        P("head", None),
        P(BATCH, "head"),
    )
    return jax.shard_map(
        shards,
        mesh=fine,
        in_specs=placed,
        out_specs=(P(BATCH, "head"), P(BATCH, "head"), P(None, "head"), P("head", None)),
        check_vma=False,
    )
```

```python
import jax
import jax.numpy as jnp
from jax import lax
from jax.experimental import pallas as pl
from jax.experimental.pallas import tpu as pltpu
from jax.sharding import Mesh, PartitionSpec as P

HD = 64
EV = 1024
WIDTH = 256
OWNERS = 32
CAP = 64
ROWS = 4096
BATCH = ("z", "y", "core")
epsilon = 1e-05
F32 = jnp.float32
BF16 = jnp.bfloat16
I32 = jnp.int32


def iota(shape, axis):
    return lax.broadcasted_iota(I32, shape, axis)


def one(mask):
    return jnp.where(mask, 1.0, 0.0).astype(BF16)


def mm(a, b, ca=1, cb=0):
    return lax.dot_general(a, b, (((ca,), (cb,)), ((), ())), preferred_element_type=F32)


def low(x):
    return x.astype(F32).astype(BF16)


def call(body, outs, memory=(), far=(), far_outs=(), scratch=(), us=1.0, mib=60):
    spec = pl.BlockSpec(memory_space=pltpu.VMEM)
    smem = pl.BlockSpec(memory_space=pltpu.SMEM)
    hbm = pl.BlockSpec(memory_space=pl.ANY)
    single = not isinstance(outs, (tuple, list))
    out_list = [outs] if single else list(outs)

    def run(*args):
        in_specs = [
            smem if i in memory else hbm if i in far else spec for i in range(len(args))
        ]
        result = pl.pallas_call(
            body,
            out_shape=out_list,
            in_specs=in_specs,
            out_specs=[hbm if i in far_outs else spec for i in range(len(out_list))],
            scratch_shapes=list(scratch),
            compiler_params=pltpu.CompilerParams(vmem_limit_bytes=mib * 2**20),
            cost_estimate=pl.CostEstimate(
                flops=int(us * 2e8), bytes_accessed=int(us * 3.6e6), transcendentals=0
            ),
        )(*args)
        return result[0] if single else result

    return run


def sds(shape, dtype):
    return jax.ShapeDtypeStruct(shape, dtype)


def route_body(length_ref, slot_ref, ids_ref, rows_ref, out_ref):
    ids = ids_ref[...]
    high, lane = ids >> 7, ids & 127
    table = rows_ref[...]
    pieces = jnp.concatenate([low(table & 255), low((table >> 8) & 255), low(table >> 16)], axis=1)
    picked = mm(pieces, one(iota((EV, EV), 0) == high), 0, 0)
    value = picked[0:128] + 256.0 * picked[128:256] + 65536.0 * picked[256:384]
    row = jnp.sum(
        jnp.where(iota((128, EV), 0) == lane, value, 0.0), axis=0, keepdims=True
    ).astype(I32)
    owner, local = row >> 12, (row & 4095) + 1
    alive = iota((1, EV), 1) < length_ref[0]
    hits = (iota((OWNERS, EV), 0) == owner) & alive
    hit = jnp.where(hits, 1.0, 0.0)
    before = mm(hit.astype(BF16), one(iota((EV, EV), 0) < iota((EV, EV), 1)))
    arrival = jnp.sum(hit * before, axis=0, keepdims=True).astype(I32)
    parts = jnp.concatenate(
        [hit * (local & 127).astype(F32), hit * (local >> 7).astype(F32)], axis=0
    ).astype(BF16)
    asked = mm(parts, one(iota((CAP, EV), 0) == arrival), 1, 1)
    asked = (asked[0:OWNERS] + 128.0 * asked[OWNERS:]).astype(I32)
    slot = slot_ref[0]
    first = jnp.concatenate([asked, jnp.full((OWNERS, 64), slot, I32)], axis=1)
    place = jnp.where(alive, owner * CAP + arrival + 1, 0)
    packed = place[:, 0:512] + 4096 * place[:, 512:1024]
    level = iota((8, 128), 0)
    base = jnp.zeros((8, 128), I32)
    for r in range(4):
        piece = jnp.broadcast_to(packed[:, 128 * r : 128 * r + 128], (8, 128))
        base = jnp.where(level == r + 1, piece, base)
    for d in range(OWNERS):
        head_row = jnp.broadcast_to(first[d : d + 1, :], (8, 128))
        out_ref[d] = jnp.where(level == 0, head_row, jnp.where(slot == d, base, 0))


def dequant_body(table_ref, scale_ref, bias_ref, out_ref):
    pad = jnp.zeros((96, 128), F32)
    scale = jnp.concatenate([scale_ref[...], pad], axis=0).T
    bias = jnp.concatenate([bias_ref[...], pad], axis=0).T
    for b in range(32):
        rows = slice(128 * b, 128 * b + 128)
        values = table_ref[rows, :].astype(F32)
        out_ref[rows, :] = (values * scale[:, b : b + 1] + bias[:, b : b + 1]).astype(BF16)


def fetch_body(asked_ref, table_ref, rows_ref, order_ref, hot_ref):
    first = jnp.concatenate([asked_ref[h, 0:1, :] for h in range(OWNERS)], axis=0)
    slot = first[:, 64:65]
    lane = iota((OWNERS, 128), 1)
    small, large = low(first & 127), low(first >> 7)
    place = one(lane == slot)
    columns = (mm(small, place, 0, 0) + 128.0 * mm(large, place, 0, 0)).astype(I32) - 1
    even, odd = one(2 * lane == slot), one(2 * lane + 1 == slot)
    even_rows = mm(even, small, 0, 0) + 128.0 * mm(even, large, 0, 0)
    odd_rows = mm(odd, small, 0, 0) + 128.0 * mm(odd, large, 0, 0)
    order = jnp.where(iota((128, 128), 1) < 64, even_rows, pltpu.roll(odd_rows, 64, 1))
    order_ref[...] = order[0:16, :].astype(I32) - 1
    table = table_ref[...]
    for c in range(8):
        for s in range(4):
            at = 4 * c + s
            column = jnp.broadcast_to(columns[0:64, at : at + 1], (CAP, 128)).astype(jnp.int16)
            for k in range(32):
                lanes = iota((CAP, 128), 1).astype(jnp.int16) + jnp.int16(128 * k)
                hot_ref[64 * at : 64 * at + 64, 128 * k : 128 * k + 128] = jnp.where(
                    column == lanes, jnp.bfloat16(1), jnp.bfloat16(0)
                )
        rows = slice(256 * c, 256 * c + 256)
        rows_ref[rows, :] = mm(hot_ref[rows, :], table).astype(BF16)


def place_body(asked_ref, fetched_ref, top_ref, bottom_ref, place_ref):
    packed = asked_ref[0]
    for h in range(1, OWNERS):
        packed = packed + asked_ref[h]
    packed = packed[1:5, :]
    place = jnp.concatenate([packed & 4095, packed >> 12], axis=0) - 1
    place_ref[...] = place
    full = jnp.concatenate([place.astype(F32), jnp.zeros((120, 128), F32)], axis=0)
    columns = full.T.astype(I32)
    fetched = fetched_ref[...]
    for b in range(8):
        hot = one(iota((128, OWNERS * CAP), 1) == columns[:, b : b + 1])
        out_ref = top_ref if b < 4 else bottom_ref
        at = 128 * (b % 4)
        out_ref[at : at + 128, :] = mm(hot, fetched).astype(BF16)


def head_tiles(act_ref, h):
    gates_values = act_ref[:, 256 * h : 256 * h + 128].astype(F32)
    query_key = act_ref[:, 256 * h + 128 : 256 * h + 256].astype(F32)
    lower = iota((EV, 128), 1) < 64
    if h % 2 == 0:
        value = jnp.where(lower, pltpu.roll(gates_values, 64, 1), 0.0)
        gate = jnp.where(lower, gates_values, 0.0)
    else:
        value = jnp.where(lower, 0.0, gates_values)
        gate = jnp.where(lower, 0.0, pltpu.roll(gates_values, 64, 1))
    key = jnp.where(lower, pltpu.roll(query_key, 64, 1), 0.0)
    return query_key, key, value, gate


def forward_body(
    me_ref,
    own_a,
    own_b,
    left_a,
    left_b,
    right_a,
    right_b,
    far_a,
    far_b,
    weight_hbm,
    gg_hbm,
    normed_hbm,
    act_hbm,
    slope_hbm,
    istd_ref,
    att_ref,
    stats_ref,
    wt_ref,
    weight_ref,
    gg_ref,
    normed_ref,
    act_ref,
    slope_ref,
    sems,
):
    weight_copy = pltpu.make_async_copy(weight_hbm, weight_ref, sems.at[0])
    weight_copy.start()
    gg_copy = pltpu.make_async_copy(gg_hbm, gg_ref, sems.at[1])
    gg_copy.start()
    me = me_ref[0]
    halves = ((own_a, right_a, far_a, left_a), (own_b, right_b, far_b, left_b))
    for b in range(4):
        rows = slice(256 * b, 256 * b + 256)
        inner = slice(256 * (b % 2), 256 * (b % 2) + 256)
        x = [ref[inner, :].astype(F32) for ref in halves[b // 2]]
        mean = sum(jnp.sum(v, axis=1, keepdims=True) for v in x) / 1024.0
        x = [v - mean for v in x]
        spread = sum(jnp.sum(v * v, axis=1, keepdims=True) for v in x) / 1024.0
        inverse = lax.rsqrt(spread + epsilon)
        istd_ref[rows, :] = inverse
        for r in range(4):
            at = pl.multiple_of(256 * ((me + r) & 3), 256)
            normed_ref[rows, pl.ds(at, 256)] = (x[r] * inverse).astype(BF16)
        if b == 0:
            weight_copy.wait()
        half = 0.5 * mm(normed_ref[rows, :], weight_ref[...])
        t = jnp.tanh(half)
        act_ref[rows, :] = (half + half * t).astype(BF16)
        slope_ref[rows, :] = (0.5 * (1.0 + t) * (1.0 + half * (1.0 - t))).astype(BF16)
    copies = [
        pltpu.make_async_copy(normed_ref, normed_hbm, sems.at[2]),
        pltpu.make_async_copy(act_ref, act_hbm, sems.at[3]),
        pltpu.make_async_copy(slope_ref, slope_hbm, sems.at[4]),
    ]
    for copy in copies:
        copy.start()
    causal = iota((256, 256), 0) >= iota((256, 256), 1)
    gates = []
    for pair in range(2):
        gate_pair = None
        for h in (2 * pair, 2 * pair + 1):
            query_key, key, value, gate = head_tiles(act_ref, h)
            gate_pair = gate if gate_pair is None else gate_pair + gate
            left = (query_key * (1.0 / 16.0)).astype(BF16)
            key, value = key.astype(BF16), value.astype(BF16)
            for b in range(4):
                rows = slice(256 * b, 256 * b + 256)
                wt_ref[:, rows] = silu_masked(mm(left[rows], key[rows], 1, 1), causal)
                if b > 0:
                    wt_ref[:, 0 : 256 * b] = silu_masked(
                        mm(left[rows], key[0 : 256 * b], 1, 1), None
                    )
                total = mm(wt_ref[:, 0 : 256 * b + 256], value[0 : 256 * b + 256])
                cols = slice(128 * pair, 128 * pair + 128)
                if h % 2 == 0:
                    att_ref[rows, cols] = total
                else:
                    att_ref[rows, cols] += total
        gates.append(gate_pair)
    gg_copy.wait()
    att = [att_ref[:, 0:128], att_ref[:, 128:256]]
    grad = [gg_ref[:, 0:128] * gates[0], gg_ref[:, 128:256] * gates[1]]
    mean = (jnp.sum(att[0], axis=1, keepdims=True) + jnp.sum(att[1], axis=1, keepdims=True)) / 256.0
    att = [v - mean for v in att]
    spread = sum(jnp.sum(v * v, axis=1, keepdims=True) for v in att)
    first = sum(jnp.sum(v, axis=1, keepdims=True) for v in grad)
    second = sum(jnp.sum(v * w, axis=1, keepdims=True) for v, w in zip(grad, att))
    lane = iota((EV, 128), 1)
    wide = jnp.where(
        lane == 0, mean, jnp.where(lane == 1, spread, jnp.where(lane == 2, first, second))
    )
    stats_ref[...] = wide.T[0:8, :]
    for copy in copies:
        copy.wait()


def silu_masked(half, mask):
    result = half + half * jnp.tanh(half)
    if mask is not None:
        result = jnp.where(mask, result, 0.0)
    return result.astype(BF16)


def backward_body(
    me_ref,
    stats_a,
    stats_b,
    stats_c,
    stats_d,
    att_ref,
    gg_ref,
    act_ref,
    slope_hbm,
    normed_hbm,
    weight_t_hbm,
    istd_hbm,
    out_weight_hbm,
    gp_hbm,
    gated_hbm,
    mixed_hbm,
    own_ref,
    far_a,
    far_b,
    right_a,
    right_b,
    left_a,
    left_b,
    grad_ref,
    dq_ref,
    slope_ref,
    normed_ref,
    weight_t_ref,
    gp_ref,
    da_ref,
    dgate_ref,
    gated_ref,
    istd_ref,
    out_weight_ref,
    mixed_ref,
    sems,
):
    loads = [
        pltpu.make_async_copy(slope_hbm, slope_ref, sems.at[0]),
        pltpu.make_async_copy(normed_hbm, normed_ref, sems.at[1]),
        pltpu.make_async_copy(weight_t_hbm, weight_t_ref, sems.at[2]),
        pltpu.make_async_copy(istd_hbm, istd_ref, sems.at[5]),
        pltpu.make_async_copy(out_weight_hbm, out_weight_ref, sems.at[6]),
    ]
    for copy in loads:
        copy.start()
    lower = iota((EV, 128), 1) < 64
    stats = [ref[...] for ref in (stats_a, stats_b, stats_c, stats_d)]
    mean = sum(s[0:1] for s in stats) / 4.0
    spread = sum(s[1:2] + 256.0 * (s[0:1] - mean) * (s[0:1] - mean) for s in stats) / 1024.0
    inverse = lax.rsqrt(spread + epsilon)
    first = sum(s[2:3] for s in stats) / 1024.0
    second = sum(s[3:4] + (s[0:1] - mean) * s[2:3] for s in stats) * inverse / 1024.0
    wide = jnp.concatenate([mean, inverse, first, second, jnp.zeros((124, EV), F32)], axis=0).T
    mean, inverse, first, second = (wide[:, i : i + 1] for i in range(4))
    for pair in range(2):
        cols = slice(128 * pair, 128 * pair + 128)
        even = act_ref[:, 512 * pair : 512 * pair + 128].astype(F32)
        odd = act_ref[:, 512 * pair + 256 : 512 * pair + 384].astype(F32)
        gate = jnp.where(lower, even, pltpu.roll(odd, 64, 1))
        normal = (att_ref[:, cols] - mean) * inverse
        gated_ref[:, cols] = (normal * gate).astype(BF16)
        up = gg_ref[:, cols]
        dgate_ref[:, cols] = up * normal
        da_ref[:, cols] = (inverse * (up * gate - first - normal * second)).astype(BF16)
    gated_copy = pltpu.make_async_copy(gated_ref, gated_hbm, sems.at[4])
    gated_copy.start()
    loads[4].wait()
    for b in range(4):
        rows = slice(256 * b, 256 * b + 256)
        mixed_ref[rows, :] = mm(gated_ref[rows, :], out_weight_ref[...]).astype(BF16)
    mixed_copy = pltpu.make_async_copy(mixed_ref, mixed_hbm, sems.at[7])
    mixed_copy.start()
    causal = iota((256, 256), 1) >= iota((256, 256), 0)
    for h in range(4):
        pair = h // 2
        query_key, key, value, _ = head_tiles(act_ref, h)
        left = query_key * (1.0 / 16.0)
        query = jnp.where(lower, 0.0, pltpu.roll(left, 64, 1)).astype(BF16)
        left = left.astype(BF16)
        key_t = (key * (1.0 / 16.0)).T.astype(BF16)
        key, value = key.astype(BF16), value.astype(BF16)
        da = da_ref[:, 128 * pair : 128 * pair + 128]
        dq_ref[...] = jnp.zeros_like(dq_ref)
        dks, dvs = [], []
        for b in range(4):
            keys = slice(256 * b, 256 * b + 256)
            dk = dv = 0.0
            spans = [(keys, causal)]
            if b < 3:
                spans.append((slice(256 * b + 256, EV), None))
            for span, mask in spans:
                half = mm(key[keys], left[span], 1, 1)
                t = jnp.tanh(half)
                weights = half + half * t
                up = mm(value[keys], da[span], 1, 1)
                gs = up * ((1.0 + t) * (1.0 + half - half * t))
                if mask is not None:
                    weights = jnp.where(mask, weights, 0.0)
                    gs = jnp.where(mask, gs, 0.0)
                gs = gs.astype(BF16)
                dv = dv + mm(weights.astype(BF16), da[span])
                dk = dk + mm(gs, query[span])
                dq_ref[:, span] += mm(key_t[:, keys], gs)
            dks.append(dk)
            dvs.append(dv)
        dqk = dq_ref[...].T + jnp.concatenate(dks, axis=0)
        dv = jnp.concatenate(dvs, axis=0)
        dgate = dgate_ref[:, 128 * pair : 128 * pair + 128]
        if h % 2 == 0:
            dgv = jnp.where(lower, dgate, pltpu.roll(dv, 64, 1))
        else:
            dgv = jnp.where(lower, pltpu.roll(dgate, 64, 1), dv)
        if h == 0:
            loads[0].wait()
        a, b = slice(256 * h, 256 * h + 128), slice(256 * h + 128, 256 * h + 256)
        gp_ref[:, a] = (dgv * slope_ref[:, a].astype(F32)).astype(BF16)
        gp_ref[:, b] = (dqk * slope_ref[:, b].astype(F32)).astype(BF16)
    gp_copy = pltpu.make_async_copy(gp_ref, gp_hbm, sems.at[3])
    gp_copy.start()
    loads[1].wait()
    loads[2].wait()
    loads[3].wait()
    for b in range(4):
        rows = slice(256 * b, 256 * b + 256)
        grad = mm(gp_ref[rows, :], weight_t_ref[...])
        normed = normed_ref[rows, :].astype(F32)
        first = jnp.sum(grad, axis=1, keepdims=True) / 1024.0
        second = jnp.sum(grad * normed, axis=1, keepdims=True) / 1024.0
        grad = (istd_ref[rows, :] * (grad - first - normed * second)).astype(BF16)
        grad_ref[rows, :] = grad
    me = me_ref[0]

    def columns(r):
        return pl.ds(pl.multiple_of(256 * ((me + r) & 3), 256), 256)

    own_ref[...] = grad_ref[:, columns(0)]
    for r, top, bottom in ((1, right_a, right_b), (2, far_a, far_b), (3, left_a, left_b)):
        top[...] = grad_ref[0:512, columns(r)]
        bottom[...] = grad_ref[512:1024, columns(r)]
    gp_copy.wait()
    gated_copy.wait()
    mixed_copy.wait()


def weights_body(
    core_ref,
    normed_ref,
    gp_ref,
    gated_hbm,
    cot_hbm,
    kept_ref,
    sent_ref,
    all_ref,
    gated_ref,
    cot_ref,
    sems,
):
    loads = [
        pltpu.make_async_copy(gated_hbm, gated_ref, sems.at[0]),
        pltpu.make_async_copy(cot_hbm, cot_ref, sems.at[1]),
    ]
    for copy in loads:
        copy.start()
    for c in range(2):
        rows = slice(512 * c, 512 * c + 512)
        grad = mm(normed_ref[:, rows], gp_ref[...], 0, 0).astype(BF16)
        all_ref[c, 0:512, :] = grad
    loads[0].wait()
    loads[1].wait()
    grad = mm(gated_ref[...], cot_ref[...], 0, 0).astype(BF16)
    for c in range(2):
        all_ref[c, 512:640, :] = grad[128 * c : 128 * c + 128]
    core = core_ref[0]
    for d in range(16):
        kept_ref[d, 0:32, :] = all_ref[core, 32 * d : 32 * d + 32, :]
        kept_ref[d, 32:40, :] = all_ref[core, 512 + 8 * d : 520 + 8 * d, :]
        sent_ref[d, 0:32, :] = all_ref[1 - core, 32 * d : 32 * d + 32, :]
        sent_ref[d, 32:40, :] = all_ref[1 - core, 512 + 8 * d : 520 + 8 * d, :]


def unfold_body(core_ref, mine_ref, other_ref, proj_ref, out_ref):
    for ref, core in ((mine_ref, core_ref[0]), (other_ref, 1 - core_ref[0])):
        for d in range(16):
            at = 16 * core + d
            proj_ref[pl.ds(pl.multiple_of(32 * at, 32), 32), :] = ref[d, 0:32, :].astype(F32)
            out_ref[pl.ds(pl.multiple_of(8 * at, 8), 8), :] = ref[d, 32:40, :].astype(F32)


def return_body(cot_ref, own_ref, top_a, top_b, bottom_a, bottom_b, place_ref, out_ref):
    def added(rows, a, b):
        total = cot_ref[rows, :].astype(F32) + own_ref[rows, :].astype(F32)
        return (total + a[...].astype(F32) + b[...].astype(F32)).astype(BF16)

    total = jnp.concatenate(
        [added(slice(0, 512), top_a, top_b), added(slice(512, EV), bottom_a, bottom_b)], axis=0
    )
    place = jnp.concatenate([place_ref[b : b + 1, :] for b in range(8)], axis=1)
    for c in range(4):
        hot = one(iota((512, EV), 0) + 512 * c == place)
        out_ref[512 * c : 512 * c + 512, :] = mm(hot, total).astype(BF16)


def scatter_body(rows_ref, order_ref, out_ref):
    order = jnp.concatenate([order_ref[b : b + 1, :] for b in range(16)], axis=1)
    base = pl.program_id(0) * 512
    hot = one(iota((512, OWNERS * CAP), 0) + base == order)
    out_ref[...] = mm(hot, rows_ref[...])


def scatter(rows, order):
    return pl.pallas_call(
        scatter_body,
        grid=(8,),
        out_shape=sds((ROWS, WIDTH), F32),
        in_specs=[
            pl.BlockSpec((OWNERS * CAP, WIDTH), lambda i: (0, 0)),
            pl.BlockSpec((16, 128), lambda i: (0, 0)),
        ],
        out_specs=pl.BlockSpec((512, WIDTH), lambda i: (i, 0)),
        compiler_params=pltpu.CompilerParams(vmem_limit_bytes=40 * 2**20),
        cost_estimate=pl.CostEstimate(flops=10**9, bytes_accessed=2 * 10**7, transcendentals=0),
    )(rows, order)


def shifted(x, axis, step):
    n = lax.axis_size(axis)
    return lax.ppermute(x, axis, [(i, (i + step) % n) for i in range(n)])


def plus(a, b):
    return (a.astype(F32) + b.astype(F32)).astype(BF16)


def shards(
    item_ids,
    lengths,
    assignment,
    row_of_item,
    table_values,
    row_scale,
    row_bias,
    proj_weight,
    out_weight,
    cotangent,
):
    portion = lax.all_gather(cotangent, "head", axis=1, tiled=True)
    payload = call(route_body, sds((OWNERS, 8, 128), I32), memory=(0, 1), us=3.4)(
        lengths, assignment, item_ids, row_of_item.reshape(1024, 128)
    )
    asked = lax.all_to_all(payload, BATCH, split_axis=0, concat_axis=0, tiled=True)
    table = call(dequant_body, sds((ROWS, WIDTH), BF16), us=4.0)(
        table_values, row_scale.reshape(32, 128), row_bias.reshape(32, 128)
    )
    asked, table = lax.optimization_barrier((asked, table))
    rows, order = call(
        fetch_body,
        [sds((OWNERS * CAP, WIDTH), BF16), sds((16, 128), I32)],
        scratch=[pltpu.VMEM((OWNERS * CAP, ROWS), BF16)],
        us=8.0,
    )(asked, table)
    fetched = lax.all_to_all(
        rows.reshape(OWNERS, CAP, WIDTH), BATCH, split_axis=0, concat_axis=0, tiled=True
    ).reshape(OWNERS * CAP, WIDTH)
    grad_gated = mm(portion, out_weight, 1, 1)
    weight_t = proj_weight.T
    fetched, grad_gated, weight_t = lax.optimization_barrier((fetched, grad_gated, weight_t))
    head = lax.axis_index("head").reshape(1)
    half = sds((512, WIDTH), BF16)
    own_a, own_b, place = call(
        place_body, [half, half, sds((8, 128), I32)], us=3.4
    )(asked, fetched)
    left_a = shifted(own_a, "head", 1)
    right_b = shifted(own_b, "head", 3)
    left_b = shifted(own_b, "head", 1)
    right_a = shifted(own_a, "head", 3)
    far_a = shifted(left_a, "head", 1)
    far_b = shifted(right_b, "head", 3)
    normed, act, slope, istd, att, stats = call(
        forward_body,
        [
            sds((EV, 1024), BF16),
            sds((EV, 1024), BF16),
            sds((EV, 1024), BF16),
            sds((EV, 1), F32),
            sds((EV, WIDTH), F32),
            sds((8, EV), F32),
        ],
        memory=(0,),
        far=(9, 10),
        far_outs=(0, 1, 2),
        scratch=[
            pltpu.VMEM((256, EV), BF16),
            pltpu.VMEM((EV, 1024), BF16),
            pltpu.VMEM((EV, WIDTH), F32),
            pltpu.VMEM((EV, 1024), BF16),
            pltpu.VMEM((EV, 1024), BF16),
            pltpu.VMEM((EV, 1024), BF16),
            pltpu.SemaphoreType.DMA((5,)),
        ],
        us=10.0,
    )(
        head,
        own_a,
        own_b,
        left_a,
        left_b,
        right_a,
        right_b,
        far_a,
        far_b,
        proj_weight,
        grad_gated,
    )
    others = [shifted(stats, "head", s) for s in (1, 3, 2)]
    full = sds((EV, WIDTH), BF16)
    gp, gated, mixed, own, far_a, far_b, right_a, right_b, left_a, left_b = call(
        backward_body,
        [sds((EV, 1024), BF16), full, sds((EV, 1024), BF16), full] + [half] * 6,
        memory=(0,),
        far=(8, 9, 10, 11, 12),
        far_outs=(0, 1, 2),
        scratch=[
            pltpu.VMEM((EV, 1024), BF16),
            pltpu.VMEM((128, EV), F32),
            pltpu.VMEM((EV, 1024), BF16),
            pltpu.VMEM((EV, 1024), BF16),
            pltpu.VMEM((EV, 1024), BF16),
            pltpu.VMEM((EV, 1024), BF16),
            pltpu.VMEM((EV, WIDTH), BF16),
            pltpu.VMEM((EV, WIDTH), F32),
            pltpu.VMEM((EV, WIDTH), BF16),
            pltpu.VMEM((EV, 1), F32),
            pltpu.VMEM((WIDTH, 1024), BF16),
            pltpu.VMEM((EV, 1024), BF16),
            pltpu.SemaphoreType.DMA((8,)),
        ],
        us=20.0,
    )(head, stats, *others, att, grad_gated, act, slope, normed, weight_t, istd, out_weight)
    from_left = shifted(far_a, "head", 1)
    from_right = shifted(far_b, "head", 3)
    bottom_a = shifted(right_b, "head", 1)
    top_a = shifted(left_a, "head", 3)
    from_left, from_right, top_a, bottom_a = lax.optimization_barrier(
        (from_left, from_right, top_a, bottom_a)
    )
    right_a, left_b = plus(right_a, from_left), plus(left_b, from_right)
    mixed = lax.psum_scatter(mixed, "head", scatter_dimension=1, tiled=True)
    embedded = jnp.concatenate([own_a, own_b], axis=0)
    layer_out = (embedded.astype(F32) + mixed.astype(F32)).astype(BF16)

    core = lax.axis_index("core").reshape(1)
    kept, sent = call(
        weights_body,
        [sds((16, 40, 1024), BF16)] * 2,
        memory=(0,),
        far=(3, 4),
        scratch=[
            pltpu.VMEM((2, 640, 1024), BF16),
            pltpu.VMEM((EV, WIDTH), BF16),
            pltpu.VMEM((EV, 1024), BF16),
            pltpu.SemaphoreType.DMA((2,)),
        ],
        us=7.0,
    )(core, normed, gp, gated, portion)
    summed = plus(kept, shifted(sent, "core", 1))
    summed = lax.all_to_all(summed, ("z", "y"), split_axis=0, concat_axis=0, tiled=True)
    summed, layer_out, right_a, left_b = lax.optimization_barrier(
        (summed, layer_out, right_a, left_b)
    )
    top_b = shifted(right_a, "head", 1)
    bottom_b = shifted(left_b, "head", 3)
    piece = jnp.sum(summed.astype(F32), axis=0).astype(BF16)
    mine = lax.all_gather(piece, ("z", "y"), axis=0, tiled=True).reshape(16, 40, 1024)
    outgoing = call(return_body, sds((OWNERS * CAP, WIDTH), BF16), us=4.0)(
        cotangent, own, top_a, top_b, bottom_a, bottom_b, place
    )
    incoming = lax.all_to_all(
        outgoing.reshape(OWNERS, CAP, WIDTH), BATCH, split_axis=0, concat_axis=0, tiled=True
    ).reshape(OWNERS * CAP, WIDTH)
    row_grad = scatter(incoming, order)
    mine, row_grad = lax.optimization_barrier((mine, row_grad))
    other = shifted(mine, "core", 1)
    proj_grad, out_grad = call(
        unfold_body,
        [sds((EV, 1024), F32), sds((256, 1024), F32)],
        memory=(0,),
        us=4.0,
    )(core, mine, other)
    return (layer_out, row_grad, proj_grad, out_grad)


def solution(mesh):
    fine = Mesh(mesh.devices.reshape(4, 4, 2, 4), BATCH + ("head",))
    placed = (
        P(BATCH, None),
        P(BATCH),
        P(BATCH),
        P(),
        P(BATCH, "head"),
        P(BATCH),
        P(BATCH),
        P(None, "head"),
        P("head", None),
        P(BATCH, "head"),
    )
    return jax.shard_map(
        shards,
        mesh=fine,
        in_specs=placed,
        out_specs=(P(BATCH, "head"), P(BATCH, "head"), P(None, "head"), P("head", None)),
        check_vma=False,
    )
```

```python
import jax
import jax.numpy as jnp
from jax import lax
from jax.experimental import pallas as pl
from jax.experimental.pallas import tpu as pltpu
from jax.sharding import Mesh, PartitionSpec as P

HD = 64
EV = 1024
WIDTH = 256
OWNERS = 32
CAP = 64
ROWS = 4096
BATCH = ("z", "y", "core")
epsilon = 1e-05
F32 = jnp.float32
BF16 = jnp.bfloat16
I32 = jnp.int32


def iota(shape, axis):
    return lax.broadcasted_iota(I32, shape, axis)


def one(mask):
    return jnp.where(mask, 1.0, 0.0).astype(BF16)


def mm(a, b, ca=1, cb=0):
    return lax.dot_general(a, b, (((ca,), (cb,)), ((), ())), preferred_element_type=F32)


def low(x):
    return x.astype(F32).astype(BF16)


def call(body, outs, memory=(), far_outs=(), scratch=(), us=1.0, mib=24):
    spec = pl.BlockSpec(memory_space=pltpu.VMEM)
    smem = pl.BlockSpec(memory_space=pltpu.SMEM)
    single = not isinstance(outs, (tuple, list))
    out_list = [outs] if single else list(outs)
    out_list = [
        pltpu.HBM(o.shape, o.dtype)
        if i in far_outs
        else o
        for i, o in enumerate(out_list)
    ]

    def run(*args):
        in_specs = [smem if i in memory else spec for i in range(len(args))]
        result = pl.pallas_call(
            body,
            out_shape=out_list,
            in_specs=in_specs,
            out_specs=[spec] * len(out_list),
            scratch_shapes=list(scratch),
            compiler_params=pltpu.CompilerParams(vmem_limit_bytes=mib * 2**20),
            cost_estimate=pl.CostEstimate(
                flops=int(us * 2e8), bytes_accessed=int(us * 3.6e6), transcendentals=0
            ),
        )(*args)
        return result[0] if single else result

    return run


def sds(shape, dtype):
    return jax.ShapeDtypeStruct(shape, dtype)


def route_body(length_ref, slot_ref, ids_ref, rows_ref, out_ref):
    ids = ids_ref[...]
    high, lane = ids >> 7, ids & 127
    table = rows_ref[...]
    pieces = jnp.concatenate([low(table & 255), low((table >> 8) & 255), low(table >> 16)], axis=1)
    picked = mm(pieces, one(iota((EV, EV), 0) == high), 0, 0)
    value = picked[0:128] + 256.0 * picked[128:256] + 65536.0 * picked[256:384]
    row = jnp.sum(
        jnp.where(iota((128, EV), 0) == lane, value, 0.0), axis=0, keepdims=True
    ).astype(I32)
    owner, local = row >> 12, (row & 4095) + 1
    alive = iota((1, EV), 1) < length_ref[0]
    hits = (iota((OWNERS, EV), 0) == owner) & alive
    hit = jnp.where(hits, 1.0, 0.0)
    before = mm(hit.astype(BF16), one(iota((EV, EV), 0) < iota((EV, EV), 1)))
    arrival = jnp.sum(hit * before, axis=0, keepdims=True).astype(I32)
    parts = jnp.concatenate(
        [hit * (local & 127).astype(F32), hit * (local >> 7).astype(F32)], axis=0
    ).astype(BF16)
    asked = mm(parts, one(iota((CAP, EV), 0) == arrival), 1, 1)
    asked = (asked[0:OWNERS] + 128.0 * asked[OWNERS:]).astype(I32)
    slot = slot_ref[0]
    first = jnp.concatenate([asked, jnp.full((OWNERS, 64), slot, I32)], axis=1)
    place = jnp.where(alive, owner * CAP + arrival + 1, 0)
    packed = place[:, 0:512] + 4096 * place[:, 512:1024]
    level = iota((8, 128), 0)
    base = jnp.zeros((8, 128), I32)
    for r in range(4):
        piece = jnp.broadcast_to(packed[:, 128 * r : 128 * r + 128], (8, 128))
        base = jnp.where(level == r + 1, piece, base)
    for d in range(OWNERS):
        head_row = jnp.broadcast_to(first[d : d + 1, :], (8, 128))
        out_ref[d] = jnp.where(level == 0, head_row, jnp.where(slot == d, base, 0))


def dequant_body(table_ref, scale_ref, bias_ref, out_ref):
    pad = jnp.zeros((96, 128), F32)
    scale = jnp.concatenate([scale_ref[...], pad], axis=0).T
    bias = jnp.concatenate([bias_ref[...], pad], axis=0).T
    for b in range(32):
        rows = slice(128 * b, 128 * b + 128)
        values = table_ref[rows, :].astype(F32)
        out_ref[rows, :] = (values * scale[:, b : b + 1] + bias[:, b : b + 1]).astype(BF16)


def fetch_body(asked_ref, table_ref, rows_ref, order_ref, hot_ref):
    first = jnp.concatenate([asked_ref[h, 0:1, :] for h in range(OWNERS)], axis=0)
    slot = first[:, 64:65]
    lane = iota((OWNERS, 128), 1)
    small, large = low(first & 127), low(first >> 7)
    place = one(lane == slot)
    columns = (mm(small, place, 0, 0) + 128.0 * mm(large, place, 0, 0)).astype(I32) - 1
    even, odd = one(2 * lane == slot), one(2 * lane + 1 == slot)
    even_rows = mm(even, small, 0, 0) + 128.0 * mm(even, large, 0, 0)
    odd_rows = mm(odd, small, 0, 0) + 128.0 * mm(odd, large, 0, 0)
    order = jnp.where(iota((128, 128), 1) < 64, even_rows, pltpu.roll(odd_rows, 64, 1))
    order_ref[...] = order[0:16, :].astype(I32) - 1
    table = table_ref[...]
    for c in range(8):
        for s in range(4):
            at = 4 * c + s
            column = jnp.broadcast_to(columns[0:64, at : at + 1], (CAP, 128)).astype(jnp.int16)
            for k in range(32):
                lanes = iota((CAP, 128), 1).astype(jnp.int16) + jnp.int16(128 * k)
                hot_ref[64 * at : 64 * at + 64, 128 * k : 128 * k + 128] = jnp.where(
                    column == lanes, jnp.bfloat16(1), jnp.bfloat16(0)
                )
        rows = slice(256 * c, 256 * c + 256)
        rows_ref[rows, :] = mm(hot_ref[rows, :], table).astype(BF16)


def place_body(asked_ref, fetched_ref, top_ref, bottom_ref, place_ref):
    packed = asked_ref[0]
    for h in range(1, OWNERS):
        packed = packed + asked_ref[h]
    packed = packed[1:5, :]
    place = jnp.concatenate([packed & 4095, packed >> 12], axis=0) - 1
    place_ref[...] = place
    full = jnp.concatenate([place.astype(F32), jnp.zeros((120, 128), F32)], axis=0)
    columns = full.T.astype(I32)
    fetched = fetched_ref[...]
    for b in range(8):
        hot = one(iota((128, OWNERS * CAP), 1) == columns[:, b : b + 1])
        out_ref = top_ref if b < 4 else bottom_ref
        at = 128 * (b % 4)
        out_ref[at : at + 128, :] = mm(hot, fetched).astype(BF16)


def head_tiles(act_ref, h):
    gates_values = act_ref[:, 256 * h : 256 * h + 128].astype(F32)
    query_key = act_ref[:, 256 * h + 128 : 256 * h + 256].astype(F32)
    lower = iota((EV, 128), 1) < 64
    if h % 2 == 0:
        value = jnp.where(lower, pltpu.roll(gates_values, 64, 1), 0.0)
        gate = jnp.where(lower, gates_values, 0.0)
    else:
        value = jnp.where(lower, 0.0, gates_values)
        gate = jnp.where(lower, 0.0, pltpu.roll(gates_values, 64, 1))
    key = jnp.where(lower, pltpu.roll(query_key, 64, 1), 0.0)
    return query_key, key, value, gate


def forward_body(
    me_ref,
    own_a,
    own_b,
    left_a,
    left_b,
    right_a,
    right_b,
    far_a,
    far_b,
    weight_ref,
    gg_ref,
    normed_ref,
    act_ref,
    slope_ref,
    istd_ref,
    att_ref,
    stats_ref,
    wt_ref,
):
    me = me_ref[0]
    halves = ((own_a, right_a, far_a, left_a), (own_b, right_b, far_b, left_b))
    for b in range(4):
        rows = slice(256 * b, 256 * b + 256)
        inner = slice(256 * (b % 2), 256 * (b % 2) + 256)
        x = [ref[inner, :].astype(F32) for ref in halves[b // 2]]
        mean = sum(jnp.sum(v, axis=1, keepdims=True) for v in x) / 1024.0
        x = [v - mean for v in x]
        spread = sum(jnp.sum(v * v, axis=1, keepdims=True) for v in x) / 1024.0
        inverse = lax.rsqrt(spread + epsilon)
        istd_ref[rows, :] = inverse
        for r in range(4):
            at = pl.multiple_of(256 * ((me + r) & 3), 256)
            normed_ref[rows, pl.ds(at, 256)] = (x[r] * inverse).astype(BF16)
        half = 0.5 * mm(normed_ref[rows, :], weight_ref[...])
        t = jnp.tanh(half)
        act_ref[rows, :] = (half + half * t).astype(BF16)
        slope_ref[rows, :] = (0.5 * (1.0 + t) * (1.0 + half * (1.0 - t))).astype(BF16)
    causal = iota((256, 256), 0) >= iota((256, 256), 1)
    gates = []
    for pair in range(2):
        gate_pair = None
        for h in (2 * pair, 2 * pair + 1):
            query_key, key, value, gate = head_tiles(act_ref, h)
            gate_pair = gate if gate_pair is None else gate_pair + gate
            left = (query_key * (1.0 / 16.0)).astype(BF16)
            key, value = key.astype(BF16), value.astype(BF16)
            for b in range(4):
                rows = slice(256 * b, 256 * b + 256)
                wt_ref[:, rows] = silu_masked(mm(left[rows], key[rows], 1, 1), causal)
                if b > 0:
                    wt_ref[:, 0 : 256 * b] = silu_masked(
                        mm(left[rows], key[0 : 256 * b], 1, 1), None
                    )
                total = mm(wt_ref[:, 0 : 256 * b + 256], value[0 : 256 * b + 256])
                cols = slice(128 * pair, 128 * pair + 128)
                if h % 2 == 0:
                    att_ref[rows, cols] = total
                else:
                    att_ref[rows, cols] += total
        gates.append(gate_pair)
    att = [att_ref[:, 0:128], att_ref[:, 128:256]]
    grad = [gg_ref[:, 0:128] * gates[0], gg_ref[:, 128:256] * gates[1]]
    mean = (jnp.sum(att[0], axis=1, keepdims=True) + jnp.sum(att[1], axis=1, keepdims=True)) / 256.0
    att = [v - mean for v in att]
    spread = sum(jnp.sum(v * v, axis=1, keepdims=True) for v in att)
    first = sum(jnp.sum(v, axis=1, keepdims=True) for v in grad)
    second = sum(jnp.sum(v * w, axis=1, keepdims=True) for v, w in zip(grad, att))
    lane = iota((EV, 128), 1)
    wide = jnp.where(
        lane == 0, mean, jnp.where(lane == 1, spread, jnp.where(lane == 2, first, second))
    )
    stats_ref[...] = wide.T[0:8, :]


def silu_masked(half, mask):
    result = half + half * jnp.tanh(half)
    if mask is not None:
        result = jnp.where(mask, result, 0.0)
    return result.astype(BF16)


def backward_body(
    me_ref,
    stats_a,
    stats_b,
    stats_c,
    stats_d,
    att_ref,
    gg_ref,
    act_ref,
    slope_ref,
    normed_ref,
    weight_t_ref,
    istd_ref,
    out_weight_ref,
    cot_ref,
    kept_ref,
    sent_ref,
    mixed_ref,
    own_ref,
    far_a,
    far_b,
    right_a,
    right_b,
    left_a,
    left_b,
    grad_ref,
    dq_ref,
    da_ref,
    dgate_ref,
    gp_ref,
    gated_ref,
):
    core = me_ref[1]
    halves = ((core, kept_ref), (1 - core, sent_ref))
    lower = iota((EV, 128), 1) < 64
    stats = [ref[...] for ref in (stats_a, stats_b, stats_c, stats_d)]
    mean = sum(s[0:1] for s in stats) / 4.0
    spread = sum(s[1:2] + 256.0 * (s[0:1] - mean) * (s[0:1] - mean) for s in stats) / 1024.0
    inverse = lax.rsqrt(spread + epsilon)
    first = sum(s[2:3] for s in stats) / 1024.0
    second = sum(s[3:4] + (s[0:1] - mean) * s[2:3] for s in stats) * inverse / 1024.0
    wide = jnp.concatenate([mean, inverse, first, second, jnp.zeros((124, EV), F32)], axis=0).T
    mean, inverse, first, second = (wide[:, i : i + 1] for i in range(4))
    for pair in range(2):
        cols = slice(128 * pair, 128 * pair + 128)
        even = act_ref[:, 512 * pair : 512 * pair + 128].astype(F32)
        odd = act_ref[:, 512 * pair + 256 : 512 * pair + 384].astype(F32)
        gate = jnp.where(lower, even, pltpu.roll(odd, 64, 1))
        normal = (att_ref[:, cols] - mean) * inverse
        gated_ref[:, cols] = (normal * gate).astype(BF16)
        up = gg_ref[:, cols]
        dgate_ref[:, cols] = up * normal
        da_ref[:, cols] = (inverse * (up * gate - first - normal * second)).astype(BF16)
    for b in range(4):
        rows = slice(256 * b, 256 * b + 256)
        mixed_ref[rows, :] = mm(gated_ref[rows, :], out_weight_ref[...]).astype(BF16)
    for at, ref in halves:
        cols = pl.ds(pl.multiple_of(128 * at, 128), 128)
        grad = mm(gated_ref[:, cols], cot_ref[...], 0, 0).astype(BF16)
        for d in range(16):
            ref[d, 32:40, :] = grad[8 * d : 8 * d + 8]
    causal = iota((256, 256), 1) >= iota((256, 256), 0)
    for h in range(4):
        pair = h // 2
        query_key, key, value, _ = head_tiles(act_ref, h)
        left = query_key * (1.0 / 16.0)
        query = jnp.where(lower, 0.0, pltpu.roll(left, 64, 1)).astype(BF16)
        left = left.astype(BF16)
        key_t = (key * (1.0 / 16.0)).T.astype(BF16)
        key, value = key.astype(BF16), value.astype(BF16)
        da = da_ref[:, 128 * pair : 128 * pair + 128]
        dq_ref[...] = jnp.zeros_like(dq_ref)
        dks, dvs = [], []
        for b in range(4):
            keys = slice(256 * b, 256 * b + 256)
            dk = dv = 0.0
            spans = [(keys, causal)]
            if b < 3:
                spans.append((slice(256 * b + 256, EV), None))
            for span, mask in spans:
                half = mm(key[keys], left[span], 1, 1)
                t = jnp.tanh(half)
                weights = half + half * t
                up = mm(value[keys], da[span], 1, 1)
                gs = up * ((1.0 + t) * (1.0 + half - half * t))
                if mask is not None:
                    weights = jnp.where(mask, weights, 0.0)
                    gs = jnp.where(mask, gs, 0.0)
                gs = gs.astype(BF16)
                dv = dv + mm(weights.astype(BF16), da[span])
                dk = dk + mm(gs, query[span])
                dq_ref[:, span] += mm(key_t[:, keys], gs)
            dks.append(dk)
            dvs.append(dv)
        dqk = dq_ref[...].T + jnp.concatenate(dks, axis=0)
        dv = jnp.concatenate(dvs, axis=0)
        dgate = dgate_ref[:, 128 * pair : 128 * pair + 128]
        if h % 2 == 0:
            dgv = jnp.where(lower, dgate, pltpu.roll(dv, 64, 1))
        else:
            dgv = jnp.where(lower, pltpu.roll(dgate, 64, 1), dv)
        a, b = slice(256 * h, 256 * h + 128), slice(256 * h + 128, 256 * h + 256)
        gp_ref[:, a] = (dgv * slope_ref[:, a].astype(F32)).astype(BF16)
        gp_ref[:, b] = (dqk * slope_ref[:, b].astype(F32)).astype(BF16)
    for b in range(4):
        rows = slice(256 * b, 256 * b + 256)
        grad = mm(gp_ref[rows, :], weight_t_ref[...])
        normed = normed_ref[rows, :].astype(F32)
        first = jnp.sum(grad, axis=1, keepdims=True) / 1024.0
        second = jnp.sum(grad * normed, axis=1, keepdims=True) / 1024.0
        grad = (istd_ref[rows, :] * (grad - first - normed * second)).astype(BF16)
        grad_ref[rows, :] = grad
    me = me_ref[0]

    def columns(r):
        return pl.ds(pl.multiple_of(256 * ((me + r) & 3), 256), 256)

    own_ref[...] = grad_ref[:, columns(0)]
    for r, top, bottom in ((1, right_a, right_b), (2, far_a, far_b), (3, left_a, left_b)):
        top[...] = grad_ref[0:512, columns(r)]
        bottom[...] = grad_ref[512:1024, columns(r)]
    for at, ref in halves:
        cols = pl.ds(pl.multiple_of(512 * at, 512), 512)
        grad = mm(normed_ref[:, cols], gp_ref[...], 0, 0).astype(BF16)
        for d in range(16):
            ref[d, 0:32, :] = grad[32 * d : 32 * d + 32]


def unfold_body(place_ref, *refs):
    chunks, (proj_ref, out_ref) = refs[:8], refs[8:]
    core, y, z = place_ref[1], place_ref[2], place_ref[3]
    for c in range(2):
        for dy in range(4):
            for dz in range(4):
                at = 16 * (core ^ c) + 4 * ((z - dz) & 3) + ((y - dy) & 3)
                rows = chunks[4 * c + dy][dz].astype(F32)
                proj_ref[pl.ds(pl.multiple_of(32 * at, 32), 32), :] = rows[0:32]
                out_ref[pl.ds(pl.multiple_of(8 * at, 8), 8), :] = rows[32:40]


def return_body(cot_ref, own_ref, top_a, top_b, bottom_a, bottom_b, place_ref, out_ref):
    def added(rows, a, b):
        total = cot_ref[rows, :].astype(F32) + own_ref[rows, :].astype(F32)
        return (total + a[...].astype(F32) + b[...].astype(F32)).astype(BF16)

    total = jnp.concatenate(
        [added(slice(0, 512), top_a, top_b), added(slice(512, EV), bottom_a, bottom_b)], axis=0
    )
    place = jnp.concatenate([place_ref[b : b + 1, :] for b in range(8)], axis=1)
    for c in range(4):
        hot = one(iota((512, EV), 0) + 512 * c == place)
        out_ref[512 * c : 512 * c + 512, :] = mm(hot, total).astype(BF16)


def scatter_body(rows_ref, order_ref, out_ref):
    order = jnp.concatenate([order_ref[b : b + 1, :] for b in range(16)], axis=1)
    base = pl.program_id(0) * 512
    hot = one(iota((512, OWNERS * CAP), 0) + base == order)
    out_ref[...] = mm(hot, rows_ref[...])


def scatter(rows, order):
    return pl.pallas_call(
        scatter_body,
        grid=(8,),
        out_shape=sds((ROWS, WIDTH), F32),
        in_specs=[
            pl.BlockSpec((OWNERS * CAP, WIDTH), lambda i: (0, 0)),
            pl.BlockSpec((16, 128), lambda i: (0, 0)),
        ],
        out_specs=pl.BlockSpec((512, WIDTH), lambda i: (i, 0)),
        compiler_params=pltpu.CompilerParams(vmem_limit_bytes=24 * 2**20),
        cost_estimate=pl.CostEstimate(flops=10**9, bytes_accessed=2 * 10**7, transcendentals=0),
    )(rows, order)


def shifted(x, axis, step):
    n = lax.axis_size(axis)
    return lax.ppermute(x, axis, [(i, (i + step) % n) for i in range(n)])


def plus(a, b):
    return (a.astype(F32) + b.astype(F32)).astype(BF16)


def shards(
    item_ids,
    lengths,
    assignment,
    row_of_item,
    table_values,
    row_scale,
    row_bias,
    proj_weight,
    out_weight,
    cotangent,
):
    where = jnp.stack([lax.axis_index(a) for a in ("head", "core", "y", "z")])
    portion = lax.all_gather(cotangent, "head", axis=1, tiled=True)
    payload = call(route_body, sds((OWNERS, 8, 128), I32), memory=(0, 1), us=3.4, mib=14)(
        lengths, assignment, item_ids, row_of_item.reshape(1024, 128)
    )
    asked = lax.all_to_all(payload, BATCH, split_axis=0, concat_axis=0, tiled=True)
    table = call(dequant_body, sds((ROWS, WIDTH), BF16), us=4.0, mib=10)(
        table_values, row_scale.reshape(32, 128), row_bias.reshape(32, 128)
    )
    asked, table = lax.optimization_barrier((asked, table))
    rows, order = call(
        fetch_body,
        [sds((OWNERS * CAP, WIDTH), BF16), sds((16, 128), I32)],
        scratch=[pltpu.VMEM((OWNERS * CAP, ROWS), BF16)],
        us=8.0,
        mib=32,
    )(asked, table)
    fetched = lax.all_to_all(
        rows.reshape(OWNERS, CAP, WIDTH), BATCH, split_axis=0, concat_axis=0, tiled=True
    ).reshape(OWNERS * CAP, WIDTH)
    grad_gated = mm(portion, out_weight, 1, 1)
    weight_t = proj_weight.T
    fetched, grad_gated, weight_t, where = lax.optimization_barrier(
        (fetched, grad_gated, weight_t, where)
    )
    half = sds((512, WIDTH), BF16)
    own_a, own_b, place = call(
        place_body, [half, half, sds((8, 128), I32)], us=3.4, mib=14
    )(asked, fetched)
    left_a = shifted(own_a, "head", 1)
    right_b = shifted(own_b, "head", 3)
    left_b = shifted(own_b, "head", 1)
    right_a = shifted(own_a, "head", 3)
    far_a = shifted(left_a, "head", 1)
    far_b = shifted(right_b, "head", 3)
    normed, act, slope, istd, att, stats = call(
        forward_body,
        [
            sds((EV, 1024), BF16),
            sds((EV, 1024), BF16),
            sds((EV, 1024), BF16),
            sds((EV, 1), F32),
            sds((EV, WIDTH), F32),
            sds((8, EV), F32),
        ],
        memory=(0,),
        scratch=[pltpu.VMEM((256, EV), BF16)],
        us=10.0,
        mib=28,
    )(
        where,
        own_a,
        own_b,
        left_a,
        left_b,
        right_a,
        right_b,
        far_a,
        far_b,
        proj_weight,
        grad_gated,
    )
    others = [shifted(stats, "head", s) for s in (1, 3, 2)]
    full = sds((EV, WIDTH), BF16)
    piece = sds((16, 40, 1024), BF16)
    kept, sent, mixed, own, far_a, far_b, right_a, right_b, left_a, left_b = call(
        backward_body,
        [piece, piece, sds((EV, 1024), BF16), full] + [half] * 6,
        memory=(0,),
        far_outs=(2, 3, 4, 5, 6, 7, 8, 9),
        scratch=[
            pltpu.VMEM((EV, 1024), BF16),
            pltpu.VMEM((128, EV), F32),
            pltpu.VMEM((EV, WIDTH), BF16),
            pltpu.VMEM((EV, WIDTH), F32),
            pltpu.VMEM((EV, 1024), BF16),
            pltpu.VMEM((EV, WIDTH), BF16),
        ],
        mib=32,
        us=20.0,
    )(
        where,
        stats,
        *others,
        att,
        grad_gated,
        act,
        slope,
        normed,
        weight_t,
        istd,
        out_weight,
        portion,
    )
    from_left = shifted(far_a, "head", 1)
    from_right = shifted(far_b, "head", 3)
    bottom_a = shifted(right_b, "head", 1)
    top_a = shifted(left_a, "head", 3)
    from_left, from_right, top_a, bottom_a = lax.optimization_barrier(
        (from_left, from_right, top_a, bottom_a)
    )
    right_a, left_b = plus(right_a, from_left), plus(left_b, from_right)
    summed = plus(kept, shifted(sent, "core", 1))
    summed = lax.all_to_all(summed, ("z", "y"), split_axis=0, concat_axis=0, tiled=True)
    summed, right_a, left_b = lax.optimization_barrier((summed, right_a, left_b))
    top_b = shifted(right_a, "head", 1)
    bottom_b = shifted(left_b, "head", 3)
    piece = jnp.sum(summed.astype(F32), axis=0, keepdims=True).astype(BF16)
    strip = jnp.concatenate([piece] + [shifted(piece, "z", s) for s in (1, 2, 3)], axis=0)
    strip, top_b, bottom_b = lax.optimization_barrier((strip, top_b, bottom_b))
    mixed, top_b, bottom_b = lax.optimization_barrier((mixed, top_b, bottom_b))
    mixed = lax.psum_scatter(mixed, "head", scatter_dimension=1, tiled=True)
    embedded = jnp.concatenate([own_a, own_b], axis=0)
    layer_out = (embedded.astype(F32) + mixed.astype(F32)).astype(BF16)
    strips = [strip] + [shifted(strip, "y", s) for s in (1, 2, 3)]
    strips = strips + [shifted(v, "core", 1) for v in strips]
    outgoing = call(return_body, sds((OWNERS * CAP, WIDTH), BF16), us=4.0, mib=12)(
        cotangent, own, top_a, top_b, bottom_a, bottom_b, place
    )
    incoming = lax.all_to_all(
        outgoing.reshape(OWNERS, CAP, WIDTH), BATCH, split_axis=0, concat_axis=0, tiled=True
    ).reshape(OWNERS * CAP, WIDTH)
    row_grad = scatter(incoming, order)
    strips, row_grad = lax.optimization_barrier((strips, row_grad))
    proj_grad, out_grad = call(
        unfold_body,
        [sds((EV, 1024), F32), sds((256, 1024), F32)],
        memory=(0,),
        us=3.0,
        mib=16,
    )(where, *strips)
    return (layer_out, row_grad, proj_grad, out_grad)


def solution(mesh):
    fine = Mesh(mesh.devices.reshape(4, 4, 2, 4), BATCH + ("head",))
    placed = (
        P(BATCH, None),
        P(BATCH),
        P(BATCH),
        P(),
        P(BATCH, "head"),
        P(BATCH),
        P(BATCH),
        P(None, "head"),
        P("head", None),
        P(BATCH, "head"),
    )
    return jax.shard_map(
        shards,
        mesh=fine,
        in_specs=placed,
        out_specs=(P(BATCH, "head"), P(BATCH, "head"), P(None, "head"), P("head", None)),
        check_vma=False,
    )
```

```python
import jax
import jax.numpy as jnp
from jax import lax
from jax.experimental import pallas as pl
from jax.experimental.pallas import tpu as pltpu
from jax.sharding import Mesh, PartitionSpec as P

HD = 64
EV = 1024
WIDTH = 256
OWNERS = 32
CAP = 64
ROWS = 4096
BATCH = ("z", "y", "core")
epsilon = 1e-05
F32 = jnp.float32
BF16 = jnp.bfloat16
I32 = jnp.int32


def iota(shape, axis):
    return lax.broadcasted_iota(I32, shape, axis)


def one(mask):
    return jnp.where(mask, 1.0, 0.0).astype(BF16)


def mm(a, b, ca=1, cb=0):
    return lax.dot_general(a, b, (((ca,), (cb,)), ((), ())), preferred_element_type=F32)


def low(x):
    return x.astype(F32).astype(BF16)


def call(body, outs, memory=(), far_outs=(), scratch=(), us=1.0, mib=24):
    spec = pl.BlockSpec(memory_space=pltpu.VMEM)
    smem = pl.BlockSpec(memory_space=pltpu.SMEM)
    single = not isinstance(outs, (tuple, list))
    out_list = [outs] if single else list(outs)
    out_list = [
        pltpu.HBM(o.shape, o.dtype)
        if i in far_outs
        else o
        for i, o in enumerate(out_list)
    ]

    def run(*args):
        in_specs = [smem if i in memory else spec for i in range(len(args))]
        result = pl.pallas_call(
            body,
            out_shape=out_list,
            in_specs=in_specs,
            out_specs=[spec] * len(out_list),
            scratch_shapes=list(scratch),
            compiler_params=pltpu.CompilerParams(vmem_limit_bytes=mib * 2**20),
            cost_estimate=pl.CostEstimate(
                flops=int(us * 2e8), bytes_accessed=int(us * 3.6e6), transcendentals=0
            ),
        )(*args)
        return result[0] if single else result

    return run


def sds(shape, dtype):
    return jax.ShapeDtypeStruct(shape, dtype)


def route_body(length_ref, slot_ref, ids_ref, rows_ref, out_ref):
    ids = ids_ref[...]
    high, lane = ids >> 7, ids & 127
    table = rows_ref[...]
    pieces = jnp.concatenate([low(table & 255), low((table >> 8) & 255), low(table >> 16)], axis=1)
    picked = mm(pieces, one(iota((EV, EV), 0) == high), 0, 0)
    value = picked[0:128] + 256.0 * picked[128:256] + 65536.0 * picked[256:384]
    row = jnp.sum(
        jnp.where(iota((128, EV), 0) == lane, value, 0.0), axis=0, keepdims=True
    ).astype(I32)
    owner, local = row >> 12, (row & 4095) + 1
    alive = iota((1, EV), 1) < length_ref[0]
    hits = (iota((OWNERS, EV), 0) == owner) & alive
    hit = jnp.where(hits, 1.0, 0.0)
    before = mm(hit.astype(BF16), one(iota((EV, EV), 0) < iota((EV, EV), 1)))
    arrival = jnp.sum(hit * before, axis=0, keepdims=True).astype(I32)
    parts = jnp.concatenate(
        [hit * (local & 127).astype(F32), hit * (local >> 7).astype(F32)], axis=0
    ).astype(BF16)
    asked = mm(parts, one(iota((CAP, EV), 0) == arrival), 1, 1)
    asked = (asked[0:OWNERS] + 128.0 * asked[OWNERS:]).astype(I32)
    slot = slot_ref[0]
    first = jnp.concatenate([asked, jnp.full((OWNERS, 64), slot, I32)], axis=1)
    place = jnp.where(alive, owner * CAP + arrival + 1, 0)
    packed = place[:, 0:512] + 4096 * place[:, 512:1024]
    level = iota((8, 128), 0)
    base = jnp.zeros((8, 128), I32)
    for r in range(4):
        piece = jnp.broadcast_to(packed[:, 128 * r : 128 * r + 128], (8, 128))
        base = jnp.where(level == r + 1, piece, base)
    for d in range(OWNERS):
        head_row = jnp.broadcast_to(first[d : d + 1, :], (8, 128))
        out_ref[d] = jnp.where(level == 0, head_row, jnp.where(slot == d, base, 0))


def dequant_body(table_ref, scale_ref, bias_ref, out_ref):
    pad = jnp.zeros((96, 128), F32)
    scale = jnp.concatenate([scale_ref[...], pad], axis=0).T
    bias = jnp.concatenate([bias_ref[...], pad], axis=0).T
    for b in range(32):
        rows = slice(128 * b, 128 * b + 128)
        values = table_ref[rows, :].astype(F32)
        out_ref[rows, :] = (values * scale[:, b : b + 1] + bias[:, b : b + 1]).astype(BF16)


def fetch_body(asked_ref, table_ref, rows_ref, order_ref, hot_ref):
    first = jnp.concatenate([asked_ref[h, 0:1, :] for h in range(OWNERS)], axis=0)
    slot = first[:, 64:65]
    lane = iota((OWNERS, 128), 1)
    small, large = low(first & 127), low(first >> 7)
    place = one(lane == slot)
    columns = (mm(small, place, 0, 0) + 128.0 * mm(large, place, 0, 0)).astype(I32) - 1
    even, odd = one(2 * lane == slot), one(2 * lane + 1 == slot)
    even_rows = mm(even, small, 0, 0) + 128.0 * mm(even, large, 0, 0)
    odd_rows = mm(odd, small, 0, 0) + 128.0 * mm(odd, large, 0, 0)
    order = jnp.where(iota((128, 128), 1) < 64, even_rows, pltpu.roll(odd_rows, 64, 1))
    order_ref[...] = order[0:16, :].astype(I32) - 1
    table = table_ref[...]
    for c in range(8):
        for s in range(4):
            at = 4 * c + s
            column = jnp.broadcast_to(columns[0:64, at : at + 1], (CAP, 128)).astype(jnp.int16)
            for k in range(32):
                lanes = iota((CAP, 128), 1).astype(jnp.int16) + jnp.int16(128 * k)
                hot_ref[64 * at : 64 * at + 64, 128 * k : 128 * k + 128] = jnp.where(
                    column == lanes, jnp.bfloat16(1), jnp.bfloat16(0)
                )
        rows = slice(256 * c, 256 * c + 256)
        rows_ref[rows, :] = mm(hot_ref[rows, :], table).astype(BF16)


def place_body(asked_ref, fetched_ref, top_ref, bottom_ref, place_ref):
    packed = asked_ref[0]
    for h in range(1, OWNERS):
        packed = packed + asked_ref[h]
    packed = packed[1:5, :]
    place = jnp.concatenate([packed & 4095, packed >> 12], axis=0) - 1
    place_ref[...] = place
    full = jnp.concatenate([place.astype(F32), jnp.zeros((120, 128), F32)], axis=0)
    columns = full.T.astype(I32)
    fetched = fetched_ref[...]
    for b in range(8):
        hot = one(iota((128, OWNERS * CAP), 1) == columns[:, b : b + 1])
        out_ref = top_ref if b < 4 else bottom_ref
        at = 128 * (b % 4)
        out_ref[at : at + 128, :] = mm(hot, fetched).astype(BF16)


def head_tiles(act_ref, h):
    gates_values = act_ref[:, 256 * h : 256 * h + 128].astype(F32)
    query_key = act_ref[:, 256 * h + 128 : 256 * h + 256].astype(F32)
    lower = iota((EV, 128), 1) < 64
    if h % 2 == 0:
        value = jnp.where(lower, pltpu.roll(gates_values, 64, 1), 0.0)
        gate = jnp.where(lower, gates_values, 0.0)
    else:
        value = jnp.where(lower, 0.0, gates_values)
        gate = jnp.where(lower, 0.0, pltpu.roll(gates_values, 64, 1))
    key = jnp.where(lower, pltpu.roll(query_key, 64, 1), 0.0)
    return query_key, key, value, gate


def forward_body(
    me_ref,
    own_a,
    own_b,
    left_a,
    left_b,
    right_a,
    right_b,
    far_a,
    far_b,
    weight_ref,
    gg_ref,
    normed_ref,
    act_ref,
    slope_ref,
    istd_ref,
    att_ref,
    stats_ref,
    wt_ref,
):
    me = me_ref[0]
    halves = ((own_a, right_a, far_a, left_a), (own_b, right_b, far_b, left_b))
    for b in range(4):
        rows = slice(256 * b, 256 * b + 256)
        inner = slice(256 * (b % 2), 256 * (b % 2) + 256)
        x = [ref[inner, :].astype(F32) for ref in halves[b // 2]]
        mean = sum(jnp.sum(v, axis=1, keepdims=True) for v in x) / 1024.0
        x = [v - mean for v in x]
        spread = sum(jnp.sum(v * v, axis=1, keepdims=True) for v in x) / 1024.0
        inverse = lax.rsqrt(spread + epsilon)
        istd_ref[rows, :] = inverse
        for r in range(4):
            at = pl.multiple_of(256 * ((me + r) & 3), 256)
            normed_ref[rows, pl.ds(at, 256)] = (x[r] * inverse).astype(BF16)
        half = 0.5 * mm(normed_ref[rows, :], weight_ref[...])
        t = jnp.tanh(half)
        act_ref[rows, :] = (half + half * t).astype(BF16)
        slope_ref[rows, :] = (0.5 * (1.0 + t) * (1.0 + half * (1.0 - t))).astype(BF16)
    causal = iota((256, 256), 0) >= iota((256, 256), 1)
    gates = []
    for pair in range(2):
        gate_pair = None
        for h in (2 * pair, 2 * pair + 1):
            query_key, key, value, gate = head_tiles(act_ref, h)
            gate_pair = gate if gate_pair is None else gate_pair + gate
            left = (query_key * (1.0 / 16.0)).astype(BF16)
            key, value = key.astype(BF16), value.astype(BF16)
            for b in range(4):
                rows = slice(256 * b, 256 * b + 256)
                wt_ref[:, rows] = silu_masked(mm(left[rows], key[rows], 1, 1), causal)
                if b > 0:
                    wt_ref[:, 0 : 256 * b] = silu_masked(
                        mm(left[rows], key[0 : 256 * b], 1, 1), None
                    )
                total = mm(wt_ref[:, 0 : 256 * b + 256], value[0 : 256 * b + 256])
                cols = slice(128 * pair, 128 * pair + 128)
                if h % 2 == 0:
                    att_ref[rows, cols] = total
                else:
                    att_ref[rows, cols] += total
        gates.append(gate_pair)
    att = [att_ref[:, 0:128], att_ref[:, 128:256]]
    grad = [gg_ref[:, 0:128] * gates[0], gg_ref[:, 128:256] * gates[1]]
    mean = (jnp.sum(att[0], axis=1, keepdims=True) + jnp.sum(att[1], axis=1, keepdims=True)) / 256.0
    att = [v - mean for v in att]
    spread = sum(jnp.sum(v * v, axis=1, keepdims=True) for v in att)
    first = sum(jnp.sum(v, axis=1, keepdims=True) for v in grad)
    second = sum(jnp.sum(v * w, axis=1, keepdims=True) for v, w in zip(grad, att))
    lane = iota((EV, 128), 1)
    wide = jnp.where(
        lane == 0, mean, jnp.where(lane == 1, spread, jnp.where(lane == 2, first, second))
    )
    stats_ref[...] = wide.T[0:8, :]


def silu_masked(half, mask):
    result = half + half * jnp.tanh(half)
    if mask is not None:
        result = jnp.where(mask, result, 0.0)
    return result.astype(BF16)


def backward_body(
    me_ref,
    stats_a,
    stats_b,
    stats_c,
    stats_d,
    att_ref,
    gg_ref,
    act_ref,
    slope_ref,
    normed_ref,
    weight_t_ref,
    istd_ref,
    out_weight_ref,
    cot_ref,
    kept_ref,
    sent_ref,
    mixed_ref,
    own_ref,
    far_a,
    far_b,
    right_a,
    right_b,
    left_a,
    left_b,
    grad_ref,
    dq_ref,
    da_ref,
    dgate_ref,
    gp_ref,
    gated_ref,
):
    core = me_ref[1]
    halves = ((core, kept_ref), (1 - core, sent_ref))
    lower = iota((EV, 128), 1) < 64
    stats = [ref[...] for ref in (stats_a, stats_b, stats_c, stats_d)]
    mean = sum(s[0:1] for s in stats) / 4.0
    spread = sum(s[1:2] + 256.0 * (s[0:1] - mean) * (s[0:1] - mean) for s in stats) / 1024.0
    inverse = lax.rsqrt(spread + epsilon)
    first = sum(s[2:3] for s in stats) / 1024.0
    second = sum(s[3:4] + (s[0:1] - mean) * s[2:3] for s in stats) * inverse / 1024.0
    wide = jnp.concatenate([mean, inverse, first, second, jnp.zeros((124, EV), F32)], axis=0).T
    mean, inverse, first, second = (wide[:, i : i + 1] for i in range(4))
    for pair in range(2):
        cols = slice(128 * pair, 128 * pair + 128)
        even = act_ref[:, 512 * pair : 512 * pair + 128].astype(F32)
        odd = act_ref[:, 512 * pair + 256 : 512 * pair + 384].astype(F32)
        gate = jnp.where(lower, even, pltpu.roll(odd, 64, 1))
        normal = (att_ref[:, cols] - mean) * inverse
        gated_ref[:, cols] = (normal * gate).astype(BF16)
        up = gg_ref[:, cols]
        dgate_ref[:, cols] = up * normal
        da_ref[:, cols] = (inverse * (up * gate - first - normal * second)).astype(BF16)
    for b in range(4):
        rows = slice(256 * b, 256 * b + 256)
        mixed_ref[rows, :] = mm(gated_ref[rows, :], out_weight_ref[...]).astype(BF16)
    for at, ref in halves:
        cols = pl.ds(pl.multiple_of(128 * at, 128), 128)
        grad = mm(gated_ref[:, cols], cot_ref[...], 0, 0).astype(BF16)
        for d in range(16):
            ref[d, 32:40, :] = grad[8 * d : 8 * d + 8]
    causal = iota((256, 256), 1) >= iota((256, 256), 0)
    for h in range(4):
        pair = h // 2
        query_key, key, value, _ = head_tiles(act_ref, h)
        left = query_key * (1.0 / 16.0)
        query = jnp.where(lower, 0.0, pltpu.roll(left, 64, 1)).astype(BF16)
        left = left.astype(BF16)
        key_t = (key * (1.0 / 16.0)).T.astype(BF16)
        key, value = key.astype(BF16), value.astype(BF16)
        da = da_ref[:, 128 * pair : 128 * pair + 128]
        dq_ref[...] = jnp.zeros_like(dq_ref)
        dks, dvs = [], []
        for b in range(4):
            keys = slice(256 * b, 256 * b + 256)
            dk = dv = 0.0
            spans = [(keys, causal)]
            if b < 3:
                spans.append((slice(256 * b + 256, EV), None))
            for span, mask in spans:
                half = mm(key[keys], left[span], 1, 1)
                t = jnp.tanh(half)
                weights = half + half * t
                up = mm(value[keys], da[span], 1, 1)
                gs = up * ((1.0 + t) * (1.0 + half - half * t))
                if mask is not None:
                    weights = jnp.where(mask, weights, 0.0)
                    gs = jnp.where(mask, gs, 0.0)
                gs = gs.astype(BF16)
                dv = dv + mm(weights.astype(BF16), da[span])
                dk = dk + mm(gs, query[span])
                dq_ref[:, span] += mm(key_t[:, keys], gs)
            dks.append(dk)
            dvs.append(dv)
        dqk = dq_ref[...].T + jnp.concatenate(dks, axis=0)
        dv = jnp.concatenate(dvs, axis=0)
        dgate = dgate_ref[:, 128 * pair : 128 * pair + 128]
        if h % 2 == 0:
            dgv = jnp.where(lower, dgate, pltpu.roll(dv, 64, 1))
        else:
            dgv = jnp.where(lower, pltpu.roll(dgate, 64, 1), dv)
        a, b = slice(256 * h, 256 * h + 128), slice(256 * h + 128, 256 * h + 256)
        gp_ref[:, a] = (dgv * slope_ref[:, a].astype(F32)).astype(BF16)
        gp_ref[:, b] = (dqk * slope_ref[:, b].astype(F32)).astype(BF16)
    for b in range(4):
        rows = slice(256 * b, 256 * b + 256)
        grad = mm(gp_ref[rows, :], weight_t_ref[...])
        normed = normed_ref[rows, :].astype(F32)
        first = jnp.sum(grad, axis=1, keepdims=True) / 1024.0
        second = jnp.sum(grad * normed, axis=1, keepdims=True) / 1024.0
        grad = (istd_ref[rows, :] * (grad - first - normed * second)).astype(BF16)
        grad_ref[rows, :] = grad
    me = me_ref[0]

    def columns(r):
        return pl.ds(pl.multiple_of(256 * ((me + r) & 3), 256), 256)

    own_ref[...] = grad_ref[:, columns(0)]
    for r, top, bottom in ((1, right_a, right_b), (2, far_a, far_b), (3, left_a, left_b)):
        top[...] = grad_ref[0:512, columns(r)]
        bottom[...] = grad_ref[512:1024, columns(r)]
    for at, ref in halves:
        cols = pl.ds(pl.multiple_of(512 * at, 512), 512)
        grad = mm(normed_ref[:, cols], gp_ref[...], 0, 0).astype(BF16)
        for d in range(16):
            ref[d, 0:32, :] = grad[32 * d : 32 * d + 32]


def unfold_body(place_ref, *refs):
    chunks, (proj_ref, out_ref) = refs[:10], refs[10:]
    core, y, z = place_ref[1], place_ref[2], place_ref[3]
    for c in range(2):
        own, below, above, far_a, far_b = chunks[5 * c : 5 * c + 5]
        parts = [(own, 0, 0, 4), (below, 1, 0, 4), (above, 3, 0, 4), (far_a, 2, 0, 2), (far_b, 2, 2, 4)]
        for ref, dy, first, last in parts:
            for dz in range(first, last):
                at = 16 * (core ^ c) + 4 * ((z - dz) & 3) + ((y - dy) & 3)
                rows = ref[dz - first].astype(F32)
                proj_ref[pl.ds(pl.multiple_of(32 * at, 32), 32), :] = rows[0:32]
                out_ref[pl.ds(pl.multiple_of(8 * at, 8), 8), :] = rows[32:40]


def return_body(cot_ref, own_ref, top_a, top_b, bottom_a, bottom_b, place_ref, out_ref):
    def added(rows, a, b):
        total = cot_ref[rows, :].astype(F32) + own_ref[rows, :].astype(F32)
        return (total + a[...].astype(F32) + b[...].astype(F32)).astype(BF16)

    total = jnp.concatenate(
        [added(slice(0, 512), top_a, top_b), added(slice(512, EV), bottom_a, bottom_b)], axis=0
    )
    place = jnp.concatenate([place_ref[b : b + 1, :] for b in range(8)], axis=1)
    for c in range(4):
        hot = one(iota((512, EV), 0) + 512 * c == place)
        out_ref[512 * c : 512 * c + 512, :] = mm(hot, total).astype(BF16)


def scatter_body(rows_ref, order_ref, out_ref):
    order = jnp.concatenate([order_ref[b : b + 1, :] for b in range(16)], axis=1)
    base = pl.program_id(0) * 512
    hot = one(iota((512, OWNERS * CAP), 0) + base == order)
    out_ref[...] = mm(hot, rows_ref[...])


def scatter(rows, order):
    return pl.pallas_call(
        scatter_body,
        grid=(8,),
        out_shape=sds((ROWS, WIDTH), F32),
        in_specs=[
            pl.BlockSpec((OWNERS * CAP, WIDTH), lambda i: (0, 0)),
            pl.BlockSpec((16, 128), lambda i: (0, 0)),
        ],
        out_specs=pl.BlockSpec((512, WIDTH), lambda i: (i, 0)),
        compiler_params=pltpu.CompilerParams(vmem_limit_bytes=24 * 2**20),
        cost_estimate=pl.CostEstimate(flops=10**9, bytes_accessed=2 * 10**7, transcendentals=0),
    )(rows, order)


def shifted(x, axis, step):
    n = lax.axis_size(axis)
    return lax.ppermute(x, axis, [(i, (i + step) % n) for i in range(n)])


def plus(a, b):
    return (a.astype(F32) + b.astype(F32)).astype(BF16)


def shards(
    item_ids,
    lengths,
    assignment,
    row_of_item,
    table_values,
    row_scale,
    row_bias,
    proj_weight,
    out_weight,
    cotangent,
):
    where = jnp.stack([lax.axis_index(a) for a in ("head", "core", "y", "z")])
    portion = lax.all_gather(cotangent, "head", axis=1, tiled=True)
    payload = call(route_body, sds((OWNERS, 8, 128), I32), memory=(0, 1), us=3.4, mib=60)(
        lengths, assignment, item_ids, row_of_item.reshape(1024, 128)
    )
    asked = lax.all_to_all(payload, BATCH, split_axis=0, concat_axis=0, tiled=True)
    table = call(dequant_body, sds((ROWS, WIDTH), BF16), us=4.0, mib=10)(
        table_values, row_scale.reshape(32, 128), row_bias.reshape(32, 128)
    )
    asked, table = lax.optimization_barrier((asked, table))
    rows, order = call(
        fetch_body,
        [sds((OWNERS * CAP, WIDTH), BF16), sds((16, 128), I32)],
        scratch=[pltpu.VMEM((OWNERS * CAP, ROWS), BF16)],
        us=8.0,
        mib=32,
    )(asked, table)
    fetched = lax.all_to_all(
        rows.reshape(OWNERS, CAP, WIDTH), BATCH, split_axis=0, concat_axis=0, tiled=True
    ).reshape(OWNERS * CAP, WIDTH)
    grad_gated = mm(portion, out_weight, 1, 1)
    weight_t = proj_weight.T
    fetched, grad_gated, weight_t, where = lax.optimization_barrier(
        (fetched, grad_gated, weight_t, where)
    )
    half = sds((512, WIDTH), BF16)
    own_a, own_b, place = call(
        place_body, [half, half, sds((8, 128), I32)], us=3.4, mib=14
    )(asked, fetched)
    left_a = shifted(own_a, "head", 1)
    right_b = shifted(own_b, "head", 3)
    left_b = shifted(own_b, "head", 1)
    right_a = shifted(own_a, "head", 3)
    far_a = shifted(left_a, "head", 1)
    far_b = shifted(right_b, "head", 3)
    normed, act, slope, istd, att, stats = call(
        forward_body,
        [
            sds((EV, 1024), BF16),
            sds((EV, 1024), BF16),
            sds((EV, 1024), BF16),
            sds((EV, 1), F32),
            sds((EV, WIDTH), F32),
            sds((8, EV), F32),
        ],
        memory=(0,),
        scratch=[pltpu.VMEM((256, EV), BF16)],
        us=10.0,
        mib=28,
    )(
        where,
        own_a,
        own_b,
        left_a,
        left_b,
        right_a,
        right_b,
        far_a,
        far_b,
        proj_weight,
        grad_gated,
    )
    others = [shifted(stats, "head", s) for s in (1, 3, 2)]
    full = sds((EV, WIDTH), BF16)
    piece = sds((16, 40, 1024), BF16)
    kept, sent, mixed, own, far_a, far_b, right_a, right_b, left_a, left_b = call(
        backward_body,
        [piece, piece, sds((EV, 1024), BF16), full] + [half] * 6,
        memory=(0,),
        far_outs=(2, 3, 4, 5, 6, 7, 8, 9),
        scratch=[
            pltpu.VMEM((EV, 1024), BF16),
            pltpu.VMEM((128, EV), F32),
            pltpu.VMEM((EV, WIDTH), BF16),
            pltpu.VMEM((EV, WIDTH), F32),
            pltpu.VMEM((EV, 1024), BF16),
            pltpu.VMEM((EV, WIDTH), BF16),
        ],
        mib=32,
        us=20.0,
    )(
        where,
        stats,
        *others,
        att,
        grad_gated,
        act,
        slope,
        normed,
        weight_t,
        istd,
        out_weight,
        portion,
    )
    from_left = shifted(far_a, "head", 1)
    from_right = shifted(far_b, "head", 3)
    bottom_a = shifted(right_b, "head", 1)
    top_a = shifted(left_a, "head", 3)
    from_left, from_right, top_a, bottom_a = lax.optimization_barrier(
        (from_left, from_right, top_a, bottom_a)
    )
    right_a, left_b = plus(right_a, from_left), plus(left_b, from_right)
    summed = plus(kept, shifted(sent, "core", 1))
    summed = lax.all_to_all(summed, ("z", "y"), split_axis=0, concat_axis=0, tiled=True)
    summed, right_a, left_b = lax.optimization_barrier((summed, right_a, left_b))
    top_b = shifted(right_a, "head", 1)
    bottom_b = shifted(left_b, "head", 3)
    piece = jnp.sum(summed.astype(F32), axis=0, keepdims=True).astype(BF16)
    strip = jnp.concatenate([piece] + [shifted(piece, "z", s) for s in (1, 2, 3)], axis=0)
    strip, top_b, bottom_b = lax.optimization_barrier((strip, top_b, bottom_b))
    mixed, top_b, bottom_b = lax.optimization_barrier((mixed, top_b, bottom_b))
    mixed = lax.psum_scatter(mixed, "head", scatter_dimension=1, tiled=True)
    embedded = jnp.concatenate([own_a, own_b], axis=0)
    layer_out = (embedded.astype(F32) + mixed.astype(F32)).astype(BF16)
    below, above = shifted(strip, "y", 1), shifted(strip, "y", 3)
    far = [shifted(below[0:2], "y", 1), shifted(above[2:4], "y", 3)]
    strips = [strip, below, above] + far
    outgoing = call(return_body, sds((OWNERS * CAP, WIDTH), BF16), us=4.0, mib=12)(
        cotangent, own, top_a, top_b, bottom_a, bottom_b, place
    )
    incoming = lax.all_to_all(
        outgoing.reshape(OWNERS, CAP, WIDTH), BATCH, split_axis=0, concat_axis=0, tiled=True
    ).reshape(OWNERS * CAP, WIDTH)
    row_grad = scatter(incoming, order)
    strips, row_grad, layer_out = lax.optimization_barrier((strips, row_grad, layer_out))
    strips = strips + [shifted(v, "core", 1) for v in strips]
    proj_grad, out_grad = call(
        unfold_body,
        [sds((EV, 1024), F32), sds((256, 1024), F32)],
        memory=(0,),
        us=3.0,
        mib=16,
    )(where, *strips)
    return (layer_out, row_grad, proj_grad, out_grad)


def solution(mesh):
    fine = Mesh(mesh.devices.reshape(4, 4, 2, 4), BATCH + ("head",))
    placed = (
        P(BATCH, None),
        P(BATCH),
        P(BATCH),
        P(),
        P(BATCH, "head"),
        P(BATCH),
        P(BATCH),
        P(None, "head"),
        P("head", None),
        P(BATCH, "head"),
    )
    return jax.shard_map(
        shards,
        mesh=fine,
        in_specs=placed,
        out_specs=(P(BATCH, "head"), P(BATCH, "head"), P(None, "head"), P("head", None)),
        check_vma=False,
    )
```

```python
import jax
import jax.numpy as jnp
from jax import lax
from jax.experimental import pallas as pl
from jax.experimental.pallas import tpu as pltpu
from jax.sharding import Mesh, PartitionSpec as P

HD = 64
EV = 1024
WIDTH = 256
OWNERS = 32
CAP = 64
ROWS = 4096
BATCH = ("z", "y", "core")
epsilon = 1e-05
F32 = jnp.float32
BF16 = jnp.bfloat16
I32 = jnp.int32


def iota(shape, axis):
    return lax.broadcasted_iota(I32, shape, axis)


def one(mask):
    return jnp.where(mask, 1.0, 0.0).astype(BF16)


def mm(a, b, ca=1, cb=0):
    return lax.dot_general(a, b, (((ca,), (cb,)), ((), ())), preferred_element_type=F32)


def low(x):
    return x.astype(F32).astype(BF16)


def call(body, outs, memory=(), far_outs=(), scratch=(), us=1.0, mib=24):
    spec = pl.BlockSpec(memory_space=pltpu.VMEM)
    smem = pl.BlockSpec(memory_space=pltpu.SMEM)
    single = not isinstance(outs, (tuple, list))
    out_list = [outs] if single else list(outs)
    out_list = [
        pltpu.HBM(o.shape, o.dtype)
        if i in far_outs
        else o
        for i, o in enumerate(out_list)
    ]

    def run(*args):
        in_specs = [smem if i in memory else spec for i in range(len(args))]
        result = pl.pallas_call(
            body,
            out_shape=out_list,
            in_specs=in_specs,
            out_specs=[spec] * len(out_list),
            scratch_shapes=list(scratch),
            compiler_params=pltpu.CompilerParams(vmem_limit_bytes=mib * 2**20),
            cost_estimate=pl.CostEstimate(
                flops=int(us * 2e8), bytes_accessed=int(us * 3.6e6), transcendentals=0
            ),
        )(*args)
        return result[0] if single else result

    return run


def sds(shape, dtype):
    return jax.ShapeDtypeStruct(shape, dtype)


def route_body(length_ref, slot_ref, ids_ref, rows_ref, out_ref):
    ids = ids_ref[...]
    high, lane = ids >> 7, ids & 127
    table = rows_ref[...]
    pieces = jnp.concatenate([low(table & 255), low((table >> 8) & 255), low(table >> 16)], axis=1)
    picked = mm(pieces, one(iota((EV, EV), 0) == high), 0, 0)
    value = picked[0:128] + 256.0 * picked[128:256] + 65536.0 * picked[256:384]
    row = jnp.sum(
        jnp.where(iota((128, EV), 0) == lane, value, 0.0), axis=0, keepdims=True
    ).astype(I32)
    owner, local = row >> 12, (row & 4095) + 1
    alive = iota((1, EV), 1) < length_ref[0]
    hits = (iota((OWNERS, EV), 0) == owner) & alive
    hit = jnp.where(hits, 1.0, 0.0)
    before = mm(hit.astype(BF16), one(iota((EV, EV), 0) < iota((EV, EV), 1)))
    arrival = jnp.sum(hit * before, axis=0, keepdims=True).astype(I32)
    parts = jnp.concatenate(
        [hit * (local & 127).astype(F32), hit * (local >> 7).astype(F32)], axis=0
    ).astype(BF16)
    asked = mm(parts, one(iota((CAP, EV), 0) == arrival), 1, 1)
    asked = (asked[0:OWNERS] + 128.0 * asked[OWNERS:]).astype(I32)
    slot = slot_ref[0]
    first = jnp.concatenate([asked, jnp.full((OWNERS, 64), slot, I32)], axis=1)
    place = jnp.where(alive, owner * CAP + arrival + 1, 0)
    packed = place[:, 0:512] + 4096 * place[:, 512:1024]
    level = iota((8, 128), 0)
    base = jnp.zeros((8, 128), I32)
    for r in range(4):
        piece = jnp.broadcast_to(packed[:, 128 * r : 128 * r + 128], (8, 128))
        base = jnp.where(level == r + 1, piece, base)
    for d in range(OWNERS):
        head_row = jnp.broadcast_to(first[d : d + 1, :], (8, 128))
        out_ref[d] = jnp.where(level == 0, head_row, jnp.where(slot == d, base, 0))


def dequant_body(table_ref, scale_ref, bias_ref, out_ref):
    pad = jnp.zeros((96, 128), F32)
    scale = jnp.concatenate([scale_ref[...], pad], axis=0).T
    bias = jnp.concatenate([bias_ref[...], pad], axis=0).T
    for b in range(32):
        rows = slice(128 * b, 128 * b + 128)
        values = table_ref[rows, :].astype(F32)
        out_ref[rows, :] = (values * scale[:, b : b + 1] + bias[:, b : b + 1]).astype(BF16)


def fetch_body(asked_ref, table_ref, rows_ref, order_ref, hot_ref):
    first = jnp.concatenate([asked_ref[h, 0:1, :] for h in range(OWNERS)], axis=0)
    slot = first[:, 64:65]
    lane = iota((OWNERS, 128), 1)
    small, large = low(first & 127), low(first >> 7)
    place = one(lane == slot)
    columns = (mm(small, place, 0, 0) + 128.0 * mm(large, place, 0, 0)).astype(I32) - 1
    even, odd = one(2 * lane == slot), one(2 * lane + 1 == slot)
    even_rows = mm(even, small, 0, 0) + 128.0 * mm(even, large, 0, 0)
    odd_rows = mm(odd, small, 0, 0) + 128.0 * mm(odd, large, 0, 0)
    order = jnp.where(iota((128, 128), 1) < 64, even_rows, pltpu.roll(odd_rows, 64, 1))
    order_ref[...] = order[0:16, :].astype(I32) - 1
    table = table_ref[...]
    for c in range(8):
        for s in range(4):
            at = 4 * c + s
            column = jnp.broadcast_to(columns[0:64, at : at + 1], (CAP, 128)).astype(jnp.int16)
            for k in range(32):
                lanes = iota((CAP, 128), 1).astype(jnp.int16) + jnp.int16(128 * k)
                hot_ref[64 * at : 64 * at + 64, 128 * k : 128 * k + 128] = jnp.where(
                    column == lanes, jnp.bfloat16(1), jnp.bfloat16(0)
                )
        rows = slice(256 * c, 256 * c + 256)
        rows_ref[rows, :] = mm(hot_ref[rows, :], table).astype(BF16)


def place_body(asked_ref, fetched_ref, top_ref, bottom_ref, place_ref):
    packed = asked_ref[0]
    for h in range(1, OWNERS):
        packed = packed + asked_ref[h]
    packed = packed[1:5, :]
    place = jnp.concatenate([packed & 4095, packed >> 12], axis=0) - 1
    place_ref[...] = place
    full = jnp.concatenate([place.astype(F32), jnp.zeros((120, 128), F32)], axis=0)
    columns = full.T.astype(I32)
    fetched = fetched_ref[...]
    for b in range(8):
        hot = one(iota((128, OWNERS * CAP), 1) == columns[:, b : b + 1])
        out_ref = top_ref if b < 4 else bottom_ref
        at = 128 * (b % 4)
        out_ref[at : at + 128, :] = mm(hot, fetched).astype(BF16)


def head_tiles(act_ref, h):
    gates_values = act_ref[:, 256 * h : 256 * h + 128].astype(F32)
    query_key = act_ref[:, 256 * h + 128 : 256 * h + 256].astype(F32)
    lower = iota((EV, 128), 1) < 64
    if h % 2 == 0:
        value = jnp.where(lower, pltpu.roll(gates_values, 64, 1), 0.0)
        gate = jnp.where(lower, gates_values, 0.0)
    else:
        value = jnp.where(lower, 0.0, gates_values)
        gate = jnp.where(lower, 0.0, pltpu.roll(gates_values, 64, 1))
    key = jnp.where(lower, pltpu.roll(query_key, 64, 1), 0.0)
    return query_key, key, value, gate


def forward_body(
    me_ref,
    own_a,
    own_b,
    left_a,
    left_b,
    right_a,
    right_b,
    far_a,
    far_b,
    weight_ref,
    gg_ref,
    normed_ref,
    act_ref,
    slope_ref,
    istd_ref,
    att_ref,
    stats_ref,
    wt_ref,
):
    me = me_ref[0]
    halves = ((own_a, right_a, far_a, left_a), (own_b, right_b, far_b, left_b))
    for b in range(4):
        rows = slice(256 * b, 256 * b + 256)
        inner = slice(256 * (b % 2), 256 * (b % 2) + 256)
        x = [ref[inner, :].astype(F32) for ref in halves[b // 2]]
        mean = sum(jnp.sum(v, axis=1, keepdims=True) for v in x) / 1024.0
        x = [v - mean for v in x]
        spread = sum(jnp.sum(v * v, axis=1, keepdims=True) for v in x) / 1024.0
        inverse = lax.rsqrt(spread + epsilon)
        istd_ref[rows, :] = inverse
        for r in range(4):
            at = pl.multiple_of(256 * ((me + r) & 3), 256)
            normed_ref[rows, pl.ds(at, 256)] = (x[r] * inverse).astype(BF16)
        half = 0.5 * mm(normed_ref[rows, :], weight_ref[...])
        t = jnp.tanh(half)
        act_ref[rows, :] = (half + half * t).astype(BF16)
        slope_ref[rows, :] = (0.5 * (1.0 + t) * (1.0 + half * (1.0 - t))).astype(BF16)
    causal = iota((256, 256), 0) >= iota((256, 256), 1)
    gates = []
    for pair in range(2):
        gate_pair = None
        for h in (2 * pair, 2 * pair + 1):
            query_key, key, value, gate = head_tiles(act_ref, h)
            gate_pair = gate if gate_pair is None else gate_pair + gate
            left = (query_key * (1.0 / 16.0)).astype(BF16)
            key, value = key.astype(BF16), value.astype(BF16)
            for b in range(4):
                rows = slice(256 * b, 256 * b + 256)
                wt_ref[:, rows] = silu_masked(mm(left[rows], key[rows], 1, 1), causal)
                if b > 0:
                    wt_ref[:, 0 : 256 * b] = silu_masked(
                        mm(left[rows], key[0 : 256 * b], 1, 1), None
                    )
                total = mm(wt_ref[:, 0 : 256 * b + 256], value[0 : 256 * b + 256])
                cols = slice(128 * pair, 128 * pair + 128)
                if h % 2 == 0:
                    att_ref[rows, cols] = total
                else:
                    att_ref[rows, cols] += total
        gates.append(gate_pair)
    att = [att_ref[:, 0:128], att_ref[:, 128:256]]
    grad = [gg_ref[:, 0:128] * gates[0], gg_ref[:, 128:256] * gates[1]]
    mean = (jnp.sum(att[0], axis=1, keepdims=True) + jnp.sum(att[1], axis=1, keepdims=True)) / 256.0
    att = [v - mean for v in att]
    spread = sum(jnp.sum(v * v, axis=1, keepdims=True) for v in att)
    first = sum(jnp.sum(v, axis=1, keepdims=True) for v in grad)
    second = sum(jnp.sum(v * w, axis=1, keepdims=True) for v, w in zip(grad, att))
    lane = iota((EV, 128), 1)
    wide = jnp.where(
        lane == 0, mean, jnp.where(lane == 1, spread, jnp.where(lane == 2, first, second))
    )
    stats_ref[...] = wide.T[0:8, :]


def silu_masked(half, mask):
    result = half + half * jnp.tanh(half)
    if mask is not None:
        result = jnp.where(mask, result, 0.0)
    return result.astype(BF16)


def backward_body(
    me_ref,
    stats_a,
    stats_b,
    stats_c,
    stats_d,
    att_ref,
    gg_ref,
    act_ref,
    slope_ref,
    normed_ref,
    weight_t_ref,
    istd_ref,
    out_weight_ref,
    cot_ref,
    kept_ref,
    sent_ref,
    mixed_ref,
    own_ref,
    far_a,
    far_b,
    right_a,
    right_b,
    left_a,
    left_b,
    grad_ref,
    dq_ref,
    da_ref,
    dgate_ref,
    gp_ref,
    gated_ref,
):
    core = me_ref[1]
    halves = ((core, kept_ref), (1 - core, sent_ref))
    lower = iota((EV, 128), 1) < 64
    stats = [ref[...] for ref in (stats_a, stats_b, stats_c, stats_d)]
    mean = sum(s[0:1] for s in stats) / 4.0
    spread = sum(s[1:2] + 256.0 * (s[0:1] - mean) * (s[0:1] - mean) for s in stats) / 1024.0
    inverse = lax.rsqrt(spread + epsilon)
    first = sum(s[2:3] for s in stats) / 1024.0
    second = sum(s[3:4] + (s[0:1] - mean) * s[2:3] for s in stats) * inverse / 1024.0
    wide = jnp.concatenate([mean, inverse, first, second, jnp.zeros((124, EV), F32)], axis=0).T
    mean, inverse, first, second = (wide[:, i : i + 1] for i in range(4))
    for pair in range(2):
        cols = slice(128 * pair, 128 * pair + 128)
        even = act_ref[:, 512 * pair : 512 * pair + 128].astype(F32)
        odd = act_ref[:, 512 * pair + 256 : 512 * pair + 384].astype(F32)
        gate = jnp.where(lower, even, pltpu.roll(odd, 64, 1))
        normal = (att_ref[:, cols] - mean) * inverse
        gated_ref[:, cols] = (normal * gate).astype(BF16)
        up = gg_ref[:, cols]
        dgate_ref[:, cols] = up * normal
        da_ref[:, cols] = (inverse * (up * gate - first - normal * second)).astype(BF16)
    for b in range(4):
        rows = slice(256 * b, 256 * b + 256)
        mixed_ref[rows, :] = mm(gated_ref[rows, :], out_weight_ref[...]).astype(BF16)
    for at, ref in halves:
        cols = pl.ds(pl.multiple_of(128 * at, 128), 128)
        grad = mm(gated_ref[:, cols], cot_ref[...], 0, 0).astype(BF16)
        for d in range(16):
            ref[d, 32:40, :] = grad[8 * d : 8 * d + 8]
    causal = iota((256, 256), 1) >= iota((256, 256), 0)
    for h in range(4):
        pair = h // 2
        query_key, key, value, _ = head_tiles(act_ref, h)
        left = query_key * (1.0 / 16.0)
        query = jnp.where(lower, 0.0, pltpu.roll(left, 64, 1)).astype(BF16)
        left = left.astype(BF16)
        key_t = (key * (1.0 / 16.0)).T.astype(BF16)
        key, value = key.astype(BF16), value.astype(BF16)
        da = da_ref[:, 128 * pair : 128 * pair + 128]
        dq_ref[...] = jnp.zeros_like(dq_ref)
        dks, dvs = [], []
        for b in range(4):
            keys = slice(256 * b, 256 * b + 256)
            dk = dv = 0.0
            spans = [(keys, causal)]
            if b < 3:
                spans.append((slice(256 * b + 256, EV), None))
            for span, mask in spans:
                half = mm(key[keys], left[span], 1, 1)
                t = jnp.tanh(half)
                weights = half + half * t
                up = mm(value[keys], da[span], 1, 1)
                gs = up * ((1.0 + t) * (1.0 + half - half * t))
                if mask is not None:
                    weights = jnp.where(mask, weights, 0.0)
                    gs = jnp.where(mask, gs, 0.0)
                gs = gs.astype(BF16)
                dv = dv + mm(weights.astype(BF16), da[span])
                dk = dk + mm(gs, query[span])
                dq_ref[:, span] += mm(key_t[:, keys], gs)
            dks.append(dk)
            dvs.append(dv)
        dqk = dq_ref[...].T + jnp.concatenate(dks, axis=0)
        dv = jnp.concatenate(dvs, axis=0)
        dgate = dgate_ref[:, 128 * pair : 128 * pair + 128]
        if h % 2 == 0:
            dgv = jnp.where(lower, dgate, pltpu.roll(dv, 64, 1))
        else:
            dgv = jnp.where(lower, pltpu.roll(dgate, 64, 1), dv)
        a, b = slice(256 * h, 256 * h + 128), slice(256 * h + 128, 256 * h + 256)
        gp_ref[:, a] = (dgv * slope_ref[:, a].astype(F32)).astype(BF16)
        gp_ref[:, b] = (dqk * slope_ref[:, b].astype(F32)).astype(BF16)
    for b in range(4):
        rows = slice(256 * b, 256 * b + 256)
        grad = mm(gp_ref[rows, :], weight_t_ref[...])
        normed = normed_ref[rows, :].astype(F32)
        first = jnp.sum(grad, axis=1, keepdims=True) / 1024.0
        second = jnp.sum(grad * normed, axis=1, keepdims=True) / 1024.0
        grad = (istd_ref[rows, :] * (grad - first - normed * second)).astype(BF16)
        grad_ref[rows, :] = grad
    me = me_ref[0]

    def columns(r):
        return pl.ds(pl.multiple_of(256 * ((me + r) & 3), 256), 256)

    own_ref[...] = grad_ref[:, columns(0)]
    for r, top, bottom in ((1, right_a, right_b), (2, far_a, far_b), (3, left_a, left_b)):
        top[...] = grad_ref[0:512, columns(r)]
        bottom[...] = grad_ref[512:1024, columns(r)]
    for at, ref in halves:
        cols = pl.ds(pl.multiple_of(512 * at, 512), 512)
        grad = mm(normed_ref[:, cols], gp_ref[...], 0, 0).astype(BF16)
        for d in range(16):
            ref[d, 0:32, :] = grad[32 * d : 32 * d + 32]


def unfold_body(place_ref, *refs):
    chunks, (proj_ref, out_ref) = refs[:10], refs[10:]
    core, y, z = place_ref[1], place_ref[2], place_ref[3]
    for c in range(2):
        own, below, above, far_a, far_b = chunks[5 * c : 5 * c + 5]
        parts = [(own, 0, 0, 4), (below, 1, 0, 4), (above, 3, 0, 4), (far_a, 2, 0, 2), (far_b, 2, 2, 4)]
        for ref, dy, first, last in parts:
            for dz in range(first, last):
                at = 16 * (core ^ c) + 4 * ((z - dz) & 3) + ((y - dy) & 3)
                rows = ref[dz - first].astype(F32)
                proj_ref[pl.ds(pl.multiple_of(32 * at, 32), 32), :] = rows[0:32]
                out_ref[pl.ds(pl.multiple_of(8 * at, 8), 8), :] = rows[32:40]


def return_body(cot_ref, own_ref, top_a, top_b, bottom_a, bottom_b, place_ref, out_ref):
    def added(rows, a, b):
        total = cot_ref[rows, :].astype(F32) + own_ref[rows, :].astype(F32)
        return (total + a[...].astype(F32) + b[...].astype(F32)).astype(BF16)

    total = jnp.concatenate(
        [added(slice(0, 512), top_a, top_b), added(slice(512, EV), bottom_a, bottom_b)], axis=0
    )
    place = jnp.concatenate([place_ref[b : b + 1, :] for b in range(8)], axis=1)
    for c in range(4):
        hot = one(iota((512, EV), 0) + 512 * c == place)
        out_ref[512 * c : 512 * c + 512, :] = mm(hot, total).astype(BF16)


def scatter_body(rows_ref, order_ref, out_ref):
    order = jnp.concatenate([order_ref[b : b + 1, :] for b in range(16)], axis=1)
    base = pl.program_id(0) * 512
    hot = one(iota((512, OWNERS * CAP), 0) + base == order)
    out_ref[...] = mm(hot, rows_ref[...])


def scatter(rows, order):
    return pl.pallas_call(
        scatter_body,
        grid=(8,),
        out_shape=sds((ROWS, WIDTH), F32),
        in_specs=[
            pl.BlockSpec((OWNERS * CAP, WIDTH), lambda i: (0, 0)),
            pl.BlockSpec((16, 128), lambda i: (0, 0)),
        ],
        out_specs=pl.BlockSpec((512, WIDTH), lambda i: (i, 0)),
        compiler_params=pltpu.CompilerParams(vmem_limit_bytes=24 * 2**20),
        cost_estimate=pl.CostEstimate(flops=10**9, bytes_accessed=2 * 10**7, transcendentals=0),
    )(rows, order)


def shifted(x, axis, step):
    n = lax.axis_size(axis)
    return lax.ppermute(x, axis, [(i, (i + step) % n) for i in range(n)])


def plus(a, b):
    return (a.astype(F32) + b.astype(F32)).astype(BF16)


def shards(
    item_ids,
    lengths,
    assignment,
    row_of_item,
    table_values,
    row_scale,
    row_bias,
    proj_weight,
    out_weight,
    cotangent,
):
    where = jnp.stack([lax.axis_index(a) for a in ("head", "core", "y", "z")])
    portion = lax.all_gather(cotangent, "head", axis=1, tiled=True)
    payload = call(route_body, sds((OWNERS, 8, 128), I32), memory=(0, 1), us=3.4, mib=60)(
        lengths, assignment, item_ids, row_of_item.reshape(1024, 128)
    )
    asked = lax.all_to_all(payload, BATCH, split_axis=0, concat_axis=0, tiled=True)
    table = call(dequant_body, sds((ROWS, WIDTH), BF16), us=4.0, mib=10)(
        table_values, row_scale.reshape(32, 128), row_bias.reshape(32, 128)
    )
    asked, table = lax.optimization_barrier((asked, table))
    rows, order = call(
        fetch_body,
        [sds((OWNERS * CAP, WIDTH), BF16), sds((16, 128), I32)],
        scratch=[pltpu.VMEM((OWNERS * CAP, ROWS), BF16)],
        us=8.0,
        mib=32,
    )(asked, table)
    fetched = lax.all_to_all(
        rows.reshape(OWNERS, CAP, WIDTH), BATCH, split_axis=0, concat_axis=0, tiled=True
    ).reshape(OWNERS * CAP, WIDTH)
    grad_gated = mm(portion, out_weight, 1, 1)
    weight_t = proj_weight.T
    fetched, grad_gated, weight_t, where = lax.optimization_barrier(
        (fetched, grad_gated, weight_t, where)
    )
    half = sds((512, WIDTH), BF16)
    own_a, own_b, place = call(
        place_body, [half, half, sds((8, 128), I32)], us=3.4, mib=14
    )(asked, fetched)
    left_a = shifted(own_a, "head", 1)
    right_b = shifted(own_b, "head", 3)
    left_b = shifted(own_b, "head", 1)
    right_a = shifted(own_a, "head", 3)
    far_a = shifted(left_a, "head", 1)
    far_b = shifted(right_b, "head", 3)
    normed, act, slope, istd, att, stats = call(
        forward_body,
        [
            sds((EV, 1024), BF16),
            sds((EV, 1024), BF16),
            sds((EV, 1024), BF16),
            sds((EV, 1), F32),
            sds((EV, WIDTH), F32),
            sds((8, EV), F32),
        ],
        memory=(0,),
        scratch=[pltpu.VMEM((256, EV), BF16)],
        us=10.0,
        mib=28,
    )(
        where,
        own_a,
        own_b,
        left_a,
        left_b,
        right_a,
        right_b,
        far_a,
        far_b,
        proj_weight,
        grad_gated,
    )
    others = [shifted(stats, "head", s) for s in (1, 3, 2)]
    full = sds((EV, WIDTH), BF16)
    piece = sds((16, 40, 1024), BF16)
    kept, sent, mixed, own, far_a, far_b, right_a, right_b, left_a, left_b = call(
        backward_body,
        [piece, piece, sds((EV, 1024), BF16), full] + [half] * 6,
        memory=(0,),
        far_outs=(2, 3, 4, 5, 6, 7, 8, 9),
        scratch=[
            pltpu.VMEM((EV, 1024), BF16),
            pltpu.VMEM((128, EV), F32),
            pltpu.VMEM((EV, WIDTH), BF16),
            pltpu.VMEM((EV, WIDTH), F32),
            pltpu.VMEM((EV, 1024), BF16),
            pltpu.VMEM((EV, WIDTH), BF16),
        ],
        mib=32,
        us=20.0,
    )(
        where,
        stats,
        *others,
        att,
        grad_gated,
        act,
        slope,
        normed,
        weight_t,
        istd,
        out_weight,
        portion,
    )
    from_left = shifted(far_a, "head", 1)
    from_right = shifted(far_b, "head", 3)
    bottom_a = shifted(right_b, "head", 1)
    top_a = shifted(left_a, "head", 3)
    from_left, from_right, top_a, bottom_a = lax.optimization_barrier(
        (from_left, from_right, top_a, bottom_a)
    )
    right_a, left_b = plus(right_a, from_left), plus(left_b, from_right)
    summed = plus(kept, shifted(sent, "core", 1))
    summed = lax.all_to_all(summed, ("z", "y"), split_axis=0, concat_axis=0, tiled=True)
    summed, right_a, left_b = lax.optimization_barrier((summed, right_a, left_b))
    top_b = shifted(right_a, "head", 1)
    bottom_b = shifted(left_b, "head", 3)
    piece = jnp.sum(summed.astype(F32), axis=0, keepdims=True).astype(BF16)
    strip = jnp.concatenate([piece] + [shifted(piece, "z", s) for s in (1, 2, 3)], axis=0)
    strip, top_b, bottom_b = lax.optimization_barrier((strip, top_b, bottom_b))
    mixed, top_b, bottom_b = lax.optimization_barrier((mixed, top_b, bottom_b))
    mixed = lax.psum_scatter(mixed, "head", scatter_dimension=1, tiled=True)
    embedded = jnp.concatenate([own_a, own_b], axis=0)
    layer_out = (embedded.astype(F32) + mixed.astype(F32)).astype(BF16)
    below, above = shifted(strip, "y", 1), shifted(strip, "y", 3)
    far = [shifted(below[0:2], "y", 1), shifted(above[2:4], "y", 3)]
    strips = [strip, below, above] + far
    outgoing = call(return_body, sds((OWNERS * CAP, WIDTH), BF16), us=4.0, mib=12)(
        cotangent, own, top_a, top_b, bottom_a, bottom_b, place
    )
    incoming = lax.all_to_all(
        outgoing.reshape(OWNERS, CAP, WIDTH), BATCH, split_axis=0, concat_axis=0, tiled=True
    ).reshape(OWNERS * CAP, WIDTH)
    row_grad = scatter(incoming, order)
    strips, row_grad = lax.optimization_barrier((strips, row_grad))
    strips = strips + [shifted(v, "core", 1) for v in strips]
    strips, layer_out = lax.optimization_barrier((strips, layer_out))
    proj_grad, out_grad = call(
        unfold_body,
        [sds((EV, 1024), F32), sds((256, 1024), F32)],
        memory=(0,),
        us=3.0,
        mib=16,
    )(where, *strips)
    return (layer_out, row_grad, proj_grad, out_grad)


def solution(mesh):
    fine = Mesh(mesh.devices.reshape(4, 4, 2, 4), BATCH + ("head",))
    placed = (
        P(BATCH, None),
        P(BATCH),
        P(BATCH),
        P(),
        P(BATCH, "head"),
        P(BATCH),
        P(BATCH),
        P(None, "head"),
        P("head", None),
        P(BATCH, "head"),
    )
    return jax.shard_map(
        shards,
        mesh=fine,
        in_specs=placed,
        out_specs=(P(BATCH, "head"), P(BATCH, "head"), P(None, "head"), P("head", None)),
        check_vma=False,
    )
```
